256 devices in a mesh: jpair: 8 (over z_hi, x), rows: 32 (over z_lo, y, core).
Axes of the slice: x: 4, y: 4, z: 8 (z_hi: 2, z_lo: 4; z = z_hi * 4 + z_lo), core: 2. Of those that a mesh axis runs over, the one named last changes fastest.
Arguments:
- psi_low: bfloat16 [32768, 2048], P('rows', 'jpair'), may hold values from -0.03125 to 0.03125
- psi_high: bfloat16 [32768, 2048], P('rows', 'jpair'), may hold values from -6 to 6
- dip_blocks: bfloat16 [2048, 256, 256], P('rows'), may hold values from -0.09375 to 0.09375
- block_cols: int32 [2048], replicated, may hold values from 0 to 127, as said below
Outputs:
- dipole_tile: float32 [2048, 2048], P('rows', 'jpair')
The draws below stay inside these ranges and needn't reach their ends.
Inputs may be any that keep to these rules, and one draw needn't show every extreme that they name: `block_cols`: entries 64 * s to 64 * s + 63 are the blocks stored on row shard s; block c is stored on row shard c // 4. Among the entries of one row shard, no row shard's blocks are named more than 4 times, and some row shard's blocks are named exactly 4 times by every row shard.
All inputs are finite; a program needn't handle non-finite values.
Results may differ from the reference program's by a relative error of at most 0.0029.
Values may be sent and summed in bfloat16 or wider, within the bound.
A program may use at most 128 MiB of HBM per device.

```python
import jax
import jax.numpy as jnp
from jax import lax

NV = 2048
BLK = 256
KNZ = 16
RB_DEV = 4
NB_DEV = 64
BASIS = 32768
NBLOCKS = 2048
CAP = 4
N_ROWS = 32


def draw_block_cols(key, part):
    key = jax.random.fold_in(key, 11)
    key_hot, key_order, key_local, key_place = jax.random.split(key, 4)
    slots_all = N_ROWS * CAP
    hot_owner = jax.random.randint(key_hot, (), 0, N_ROWS)

    def shuffle_slots(subkey):
        return jax.random.permutation(subkey, slots_all)

    def shuffle_places(subkey):
        return jax.random.permutation(subkey, NB_DEV)
    shuffled = jax.vmap(shuffle_slots)(jax.random.split(key_order, N_ROWS)).astype(jnp.int32)
    slot_ids = jnp.arange(slots_all, dtype=jnp.int32)
    slot_owner = slot_ids // CAP
    scores = jnp.where((slot_owner == hot_owner)[None, :], -1 - slot_ids % CAP, shuffled)
    chosen = jnp.argsort(scores, axis=1)[:, :NB_DEV].astype(jnp.int32)
    owners = chosen // CAP
    local = jax.random.randint(key_local, (N_ROWS, NB_DEV), 0, RB_DEV)
    picked = owners * RB_DEV + local
    places = jax.vmap(shuffle_places)(jax.random.split(key_place, N_ROWS)).astype(jnp.int32)
    picked = jnp.take_along_axis(picked, places, axis=1)
    return picked.reshape(-1).astype(jnp.int32)


def levels(rng, dims, cuts, low, largest):
    def one(axis_at, shards_of):
        draws = jax.random.uniform(jax.random.fold_in(jax.random.fold_in(rng, 6), axis_at), (shards_of,), jnp.float32, low / len(cuts), largest / len(cuts))
        return jnp.repeat(jnp.exp(draws), dims[axis_at] // shards_of).reshape((-1,) + (1,) * (len(dims) - axis_at - 1))

    gain = one(*cuts[0])
    for cut in cuts[1:]:
        gain = gain * one(*cut)
    return gain


def normal_values(key, shape, spread, reach, cuts=(), kind=jnp.bfloat16):
    entries = jax.random.normal(key, shape, jnp.float32) * spread
    if len(cuts) > 0:
        entries = levels(key, shape, cuts, -0.22, 0.18) * entries
    return jnp.clip(entries, min=-reach, max=reach).astype(kind)


def setup_inputs(seed: int = 0) -> dict:
    seeds = jax.random.split(jax.random.key(seed), 5)
    psi_low = normal_values(seeds[0], (BASIS, NV), BASIS ** -0.5, 0.03125, ((0, 32), (1, 8)))
    psi_high = normal_values(seeds[1], (BASIS, NV), 1.0, 6.0, ((0, 32), (1, 8)))
    dip_blocks = normal_values(seeds[2], (NBLOCKS, BLK, BLK), (BLK * KNZ) ** -0.5, 0.09375, ((0, 32),))
    block_cols = draw_block_cols(jax.random.fold_in(seeds[4], 71), 0)
    return {"psi_low": psi_low, "psi_high": psi_high, "dip_blocks": dip_blocks, "block_cols": block_cols}


def reference(psi_low, psi_high, dip_blocks, block_cols):
    row_blocks = psi_high.shape[0] // BLK
    high_blocks = psi_high.reshape(row_blocks, BLK, NV)
    dip_rows = dip_blocks.reshape(row_blocks, KNZ, BLK, BLK)
    col_rows = block_cols.reshape(row_blocks, KNZ).astype(jnp.int32)

    def row_block(pair):
        dip_row, col_row = pair
        fetched = high_blocks[col_row].astype(jnp.float32)
        return jnp.einsum("kab,kbn->an", dip_row.astype(jnp.float32), fetched, precision=lax.Precision.HIGHEST)

    applied = lax.map(row_block, (dip_rows, col_rows)).reshape(row_blocks * BLK, NV).astype(jnp.bfloat16)
    return jnp.dot(psi_low.T, applied, preferred_element_type=jnp.float32)
```

```python
import jax
import jax.numpy as jnp
from jax import lax
from jax.sharding import PartitionSpec as P

BLK = 256


def shards(psi_low, psi_high, dip_blocks, block_cols):
    own_index = lax.axis_index("rows")
    rows_dev, columns = psi_high.shape
    per_dev = dip_blocks.shape[0]
    rb_dev = rows_dev // BLK
    knz = per_dev // rb_dev
    own_list = lax.dynamic_slice_in_dim(block_cols, own_index * per_dev, per_dev)
    low = lax.all_gather(psi_low, "jpair", axis=1, tiled=True)
    high = lax.all_gather(psi_high, "rows", axis=0, tiled=True).reshape(-1, BLK, columns)
    fetched = high[own_list].reshape(rb_dev, knz, BLK, columns)
    dip = dip_blocks.reshape(rb_dev, knz, BLK, BLK)
    applied = jnp.einsum("qkab,qkbc->qac", dip, fetched, preferred_element_type=jnp.float32)
    applied = applied.reshape(rows_dev, columns).astype(jnp.bfloat16)
    partial_tile = jnp.dot(low.T, applied, preferred_element_type=jnp.float32)
    return lax.psum_scatter(partial_tile, "rows", scatter_dimension=0, tiled=True)


def solution(mesh):
    placed = (P("rows", "jpair"), P("rows", "jpair"), P("rows", None, None), P())
    return jax.shard_map(
        shards, mesh=mesh, in_specs=placed, out_specs=P("rows", "jpair"), check_vma=False
    )
```

```python
import functools

import jax
import jax.numpy as jnp
from jax import lax
from jax.experimental import pallas as pl
from jax.experimental.pallas import tpu as pltpu
from jax.sharding import PartitionSpec as P

BLK = 256
LANES = 128
MESH = pl.DeviceIdType.MESH
RING = 4
Y_TYPE = jnp.bfloat16
Z_TYPE = jnp.bfloat16


def kernel(
    cols, low, high, dip, out,
    g_a, g_b, d_buf, low_buf, low_t, applied, tile_a, tile_b, sib_buf, y_send, y_recv, z_send, z_recv,
    recv_g, send_g, recv_low, send_low, recv_sum, send_sum, local_sem,
):
    gathered = (g_a, g_b)
    tiles = (tile_a, tile_b)
    jp = lax.axis_index("jpair")
    rw = lax.axis_index("rows")
    x, zh = lax.rem(jp, RING), lax.div(jp, RING)
    c, y, z = lax.rem(rw, 2), lax.rem(lax.div(rw, 2), RING), lax.div(rw, 2 * RING)

    def rows_of(zs, ys, cs):
        return (zs * RING + ys) * 2 + cs

    def ring(v, step):
        return lax.rem(v + step + RING, RING)

    def at_rows(zs, ys, cs):
        return (jp, rows_of(zs, ys, cs))

    def at_jpair(zhs, xs):
        return (zhs * RING + xs, rw)

    right, left = at_rows(z, ring(y, 1), c), at_rows(z, ring(y, -1), c)
    sibling = at_rows(z, y, 1 - c)
    y_others = [at_rows(z, ring(y, d), c) for d in (1, 2, 3)]
    z_others = [at_rows(ring(z, d), y, c) for d in (1, 2, 3)]
    x_others = [at_jpair(zh, ring(x, d)) for d in (1, 2, 3)]
    across = at_jpair(1 - zh, x)

    barrier = pltpu.get_barrier_semaphore()
    partners = [sibling, across] + y_others + z_others + x_others
    for partner in partners:
        pl.semaphore_signal(barrier, inc=1, device_id=partner, device_id_type=MESH)
    pl.semaphore_wait(barrier, len(partners))

    last_waits = []

    def remote(src, dst, send_sem, recv_sem, target):
        return pltpu.make_async_remote_copy(
            src_ref=src, dst_ref=dst, send_sem=send_sem, recv_sem=recv_sem,
            device_id=target, device_id_type=MESH,
        )

    counts = [0, 0]

    def piece(h, r, half):
        return gathered[h].at[pl.ds(r * 4 + 2 * half, 2)]

    def send(h, r, half, target, src=None, cond=None):
        slot = counts[h]
        counts[h] += 1
        dst = piece(h, r, half)
        copy = remote(dst if src is None else src, dst, send_g.at[h, slot], recv_g.at[h, r, half], target)
        if cond is None:
            copy.start()
            last_waits.append(copy.wait_send)
        else:
            pl.when(cond)(copy.start)
            last_waits.append(lambda: pl.when(cond)(copy.wait_send))

    def arrive(h, r, half):
        ref = piece(h, r, half)
        remote(ref, ref, send_g.at[h, 0], recv_g.at[h, r, half], sibling).wait_recv()

    def own_part(h, half):
        return high.at[pl.ds(2 * half, 2), :, pl.ds(LANES * h, LANES)]

    up, down = at_rows(lax.rem(z + 1, RING), y, c), at_rows(ring(z, -1), y, c)
    sources = [z, z + 1 - 2 * lax.rem(z, 2), jnp.where(z < 2, 2, 1), jnp.where(z < 2, 3, 0)]

    def own_z(h):
        for half in (0, 1):
            send(h, rw, half, up, own_part(h, half), z < RING - 1)
            send(h, rw, half, down, own_part(h, half), z > 0)

    def own_y(h):
        for half in (0, 1):
            send(h, rw, half, right, own_part(h, half))
            send(h, rw, 1 - half, left, own_part(h, 1 - half))
        for half in (0, 1):
            send(h, rw, half, sibling, own_part(h, half))
        copy = pltpu.make_async_copy(
            high.at[:, :, pl.ds(LANES * h, LANES)], gathered[h].at[pl.ds(rw * 4, 4)], local_sem.at[h]
        )
        copy.start()
        return copy

    def from_z(h, g):
        zs = sources[g]
        r = rows_of(zs, y, c)
        below = zs < z
        onward = jnp.logical_or(jnp.logical_and(below, z < RING - 1), jnp.logical_and(zs > z, z > 0))
        target = at_rows(jnp.where(below, lax.rem(z + 1, RING), ring(z, -1)), y, c)
        for half in (0, 1):
            arrive(h, r, half)
            send(h, r, half, target, cond=onward)
            send(h, r, half, right)
            send(h, r, half, left)
            send(h, r, half, sibling)

    def from_y(h, g):
        r_left = rows_of(sources[g], ring(y, -1), c)
        r_right = rows_of(sources[g], ring(y, 1), c)
        for half in (0, 1):
            arrive(h, r_left, half)
            if half == 0:
                send(h, r_left, half, right)
            send(h, r_left, half, sibling)
            arrive(h, r_right, half)
            if half == 1:
                send(h, r_right, half, left)
            send(h, r_right, half, sibling)

    def from_far(h, g):
        r = rows_of(sources[g], ring(y, 2), c)
        for half in (0, 1):
            arrive(h, r, half)
            send(h, r, half, sibling)

    def from_sibling(h):
        for zs in range(RING):
            for ys in range(RING):
                for half in (0, 1):
                    arrive(h, rows_of(zs, ys, 1 - c), half)

    low_count = [0]

    def send_low_to(j, target, src):
        slot = low_count[0]
        low_count[0] += 1
        copy = remote(src, low_buf.at[j], send_low.at[slot], recv_low.at[j], target)
        copy.start()
        last_waits.append(copy.wait_send)

    def arrive_low(j):
        remote(low_buf.at[j], low_buf.at[j], send_low.at[0], recv_low.at[j], sibling).wait_recv()

    j_across = (1 - zh) * RING + x

    def low_start():
        for target in x_others:
            send_low_to(jp, target, low)

    def low_across():
        send_low_to(jp, across, low)

    def low_onward():
        arrive_low(j_across)
        for target in x_others:
            send_low_to(j_across, target, low_buf.at[j_across])

    def low_finish():
        own_low.wait()
        for d in (1, 2, 3):
            arrive_low(zh * RING + ring(x, d))
        for d in (1, 2, 3):
            arrive_low((1 - zh) * RING + ring(x, d))

    def low_turn(j):
        low_t[pl.ds(j * BLK, BLK), :] = low_buf[j].T

    def apply_rows(h, q):
        def some(i, total):
            for k in range(4):
                b = q * 16 + i * 4 + k
                total = total + jnp.dot(d_buf[b], gathered[h][cols[rw * 64 + b]], preferred_element_type=jnp.float32)
            return total

        total = lax.fori_loop(0, 4, some, jnp.zeros((BLK, LANES), jnp.float32))
        applied[h, pl.ds(q * BLK, BLK), :] = total.astype(jnp.bfloat16)

    def tile_rows(h, j0, n):
        def one(j, _):
            part = jnp.dot(
                low_t[pl.ds(pl.multiple_of(j * BLK, BLK), BLK), :], applied[h], preferred_element_type=jnp.float32
            )
            tiles[h][pl.ds(2 * j, 2)] = part.reshape(2, 2, 64, LANES)
            return 0

        lax.fori_loop(j0, j0 + n, one, 0)

    def sum_copy(h, k, src, dst, target):
        return remote(src, dst, send_sum.at[h, k], recv_sum.at[h, k], target)

    def sum_sibling(h):
        copy = sum_copy(h, 0, tiles[h].at[:, 1 - c], sib_buf.at[h], sibling)
        copy.start()
        return copy

    def sum_y_start(h, sib_copy):
        sib_copy.wait()
        copies = []
        for d in (2, 1, 3):
            for zs in range(RING):
                p = zs * RING + ring(y, d)
                y_send[h, d, zs] = (tiles[h][p, c] + sib_buf[h, p]).astype(Y_TYPE)
            copy = sum_copy(h, d, y_send.at[h, d], y_recv.at[h, d], y_others[d - 1])
            copy.start()
            copies.append(copy)
        return copies

    def sum_z_start(h, y_copies):
        for copy in y_copies:
            copy.wait()

        def one(zs):
            p = zs * RING + y
            total = tiles[h][p, c] + sib_buf[h, p]
            for d in (1, 2, 3):
                total = total + y_recv[h, d, zs].astype(jnp.float32)
            return total

        copies = []
        for d in (3, 2, 1):
            z_send[h, d] = one(ring(z, d)).astype(Z_TYPE)
            copy = sum_copy(h, 3 + d, z_send.at[h, d], z_recv.at[h, d], z_others[d - 1])
            copy.start()
            copies.append(copy)
        return copies, one(z)

    def sum_end(h, copies, total):
        for copy in copies:
            copy.wait()
        for d in (1, 2, 3):
            total = total + z_recv[h, d].astype(jnp.float32)
        out[:, LANES * h : LANES * (h + 1)] = total

    own_z(0)
    local_0 = own_y(0)
    low_start()
    own_low = pltpu.make_async_copy(low, low_buf.at[jp], local_sem.at[2])
    own_low.start()
    dip_copy = pltpu.make_async_copy(dip, d_buf, local_sem.at[3])
    dip_copy.start()

    from_z(0, 1)
    from_y(0, 0)
    from_z(0, 2)
    own_z(1)
    low_across()
    from_far(0, 0)
    from_z(0, 3)
    from_y(0, 1)
    from_far(0, 1)
    local_1 = own_y(1)
    from_y(0, 2)
    from_far(0, 2)
    low_onward()
    from_z(1, 1)
    from_y(0, 3)
    from_far(0, 3)
    from_sibling(0)
    local_0.wait()
    dip_copy.wait()
    from_z(1, 2)
    apply_rows(0, 0)
    from_y(1, 0)
    apply_rows(0, 1)
    from_far(1, 0)
    from_z(1, 3)
    apply_rows(0, 2)
    from_y(1, 1)
    apply_rows(0, 3)
    from_far(1, 1)
    low_finish()
    for j in range(4):
        low_turn(j)
    from_y(1, 2)
    for j in range(4, 8):
        low_turn(j)
    from_far(1, 2)
    tile_rows(0, 0, 4)
    tile_rows(0, 4, 4)
    sib_copy = sum_sibling(0)
    from_y(1, 3)
    y_copies = sum_y_start(0, sib_copy)
    from_far(1, 3)
    z_copies, mine = sum_z_start(0, y_copies)
    from_sibling(1)
    local_1.wait()
    for q in range(4):
        apply_rows(1, q)
    sum_end(0, z_copies, mine)
    tile_rows(1, 0, 8)
    sib_copy = sum_sibling(1)
    y_copies = sum_y_start(1, sib_copy)
    z_copies, mine = sum_z_start(1, y_copies)
    for wait in last_waits:
        wait()
    sum_end(1, z_copies, mine)


def shards(psi_low, psi_high, dip_blocks, block_cols):
    any_space = pl.BlockSpec(memory_space=pl.ANY)
    return pl.pallas_call(
        kernel,
        out_shape=jax.ShapeDtypeStruct((64, 256), jnp.float32),
        in_specs=[pl.BlockSpec(memory_space=pltpu.SMEM), any_space, any_space, any_space],
        out_specs=pl.BlockSpec(memory_space=pltpu.VMEM),
        scratch_shapes=[
            pltpu.VMEM((128, BLK, LANES), jnp.bfloat16),
            pltpu.VMEM((128, BLK, LANES), jnp.bfloat16),
            pltpu.VMEM((64, BLK, BLK), jnp.bfloat16),
            pltpu.VMEM((8, 1024, 256), jnp.bfloat16),
            pltpu.VMEM((2048, 1024), jnp.bfloat16),
            pltpu.VMEM((2, 1024, LANES), jnp.bfloat16),
            pltpu.VMEM((16, 2, 64, LANES), jnp.float32),
            pltpu.VMEM((16, 2, 64, LANES), jnp.float32),
            pltpu.VMEM((2, 16, 64, LANES), jnp.float32),
            pltpu.VMEM((2, 4, 4, 64, LANES), Y_TYPE),
            pltpu.VMEM((2, 4, 4, 64, LANES), Y_TYPE),
            pltpu.VMEM((2, 4, 64, LANES), Z_TYPE),
            pltpu.VMEM((2, 4, 64, LANES), Z_TYPE),
            pltpu.SemaphoreType.DMA((2, 32, 2)),
            pltpu.SemaphoreType.DMA((2, 72)),
            pltpu.SemaphoreType.DMA((8,)),
            pltpu.SemaphoreType.DMA((8,)),
            pltpu.SemaphoreType.DMA((2, 8)),
            pltpu.SemaphoreType.DMA((2, 8)),
            pltpu.SemaphoreType.DMA((4,)),
        ],
        compiler_params=pltpu.CompilerParams(
            collective_id=0, has_side_effects=True, vmem_limit_bytes=56 * 1024 * 1024
        ),
        cost_estimate=pl.CostEstimate(flops=3 * 2**30, bytes_accessed=10 * 2**20, transcendentals=0),
    )(block_cols, psi_low, psi_high.reshape(4, BLK, 256), dip_blocks)


def solution(mesh):
    placed = (P("rows", "jpair"), P("rows", "jpair"), P("rows", None, None), P())
    return jax.shard_map(
        shards, mesh=mesh, in_specs=placed, out_specs=P("rows", "jpair"), check_vma=False
    )
```

```python
import functools

import jax
import jax.numpy as jnp
from jax import lax
from jax.experimental import pallas as pl
from jax.experimental.pallas import tpu as pltpu
from jax.sharding import PartitionSpec as P

BLK = 256
LANES = 128
MESH = pl.DeviceIdType.MESH
RING = 4
Y_TYPE = jnp.bfloat16
Z_TYPE = jnp.bfloat16


def kernel(
    cols, low, high, dip, out,
    g_a, g_b, d_buf, low_buf, low_t, applied, tile_a, tile_b, sib_buf, y_send, y_recv, z_send, z_recv,
    recv_g, send_g, recv_low, send_low, recv_sum, send_sum, local_sem,
):
    gathered = (g_a, g_b)
    tiles = (tile_a, tile_b)
    jp = lax.axis_index("jpair")
    rw = lax.axis_index("rows")
    x, zh = lax.rem(jp, RING), lax.div(jp, RING)
    c, y, z = lax.rem(rw, 2), lax.rem(lax.div(rw, 2), RING), lax.div(rw, 2 * RING)

    def rows_of(zs, ys, cs):
        return (zs * RING + ys) * 2 + cs

    def ring(v, step):
        return lax.rem(v + step + RING, RING)

    def at_rows(zs, ys, cs):
        return (jp, rows_of(zs, ys, cs))

    def at_jpair(zhs, xs):
        return (zhs * RING + xs, rw)

    right, left = at_rows(z, ring(y, 1), c), at_rows(z, ring(y, -1), c)
    sibling = at_rows(z, y, 1 - c)
    y_others = [at_rows(z, ring(y, d), c) for d in (1, 2, 3)]
    z_others = [at_rows(ring(z, d), y, c) for d in (1, 2, 3)]
    x_others = [at_jpair(zh, ring(x, d)) for d in (1, 2, 3)]
    across = at_jpair(1 - zh, x)

    barrier = pltpu.get_barrier_semaphore()
    partners = [sibling, across] + y_others + z_others + x_others
    for partner in partners:
        pl.semaphore_signal(barrier, inc=1, device_id=partner, device_id_type=MESH)
    pl.semaphore_wait(barrier, len(partners))

    waits = {}

    def remote(src, dst, send_sem, recv_sem, target):
        return pltpu.make_async_remote_copy(
            src_ref=src, dst_ref=dst, send_sem=send_sem, recv_sem=recv_sem,
            device_id=target, device_id_type=MESH,
        )

    inner = jnp.logical_and(z > 0, z < RING - 1)
    slots = {}

    def piece(h, r, half, n=1):
        return gathered[h].at[pl.ds(r * 4 + 2 * half, 2 * n)]

    def send(key, h, r, half, target, src=None, n=1, cond=None):
        dst = piece(h, r, half, n)
        sem = send_g.at[h, slots.setdefault((h, key), sum(k[0] == h for k in slots))]
        copy = remote(dst if src is None else src, dst, sem, recv_g.at[h, r, half], target)
        copy.start()
        waits[(h, key)] = (n, cond)

    def arrive(h, r, half, n=1):
        ref = piece(h, r, half, n)
        remote(ref, ref, send_g.at[h, 0], recv_g.at[h, r, half], sibling).wait_recv()

    def own_part(h, half, n=1):
        return high.at[pl.ds(2 * half, 2 * n), :, pl.ds(LANES * h, LANES)]

    onward = at_rows(jnp.where(z == RING - 1, z - 1, z + 1), y, c)
    downward = at_rows(ring(z, -1), y, c)
    sources = [z, z + 1 - 2 * lax.rem(z, 2), jnp.where(z < 2, 2, 1), jnp.where(z < 2, 3, 0)]

    def own_z(h, is_inner):
        for half in (0, 1):
            send(("own_z", half, 0), h, rw, half, onward, own_part(h, half))
            if is_inner:
                send(("own_z", half, 1), h, rw, half, downward, own_part(h, half), cond=inner)

    def own_y(h, is_inner):
        for half in (0, 1):
            send(("own_y", half, 0), h, rw, half, right, own_part(h, half))
            send(("own_y", 1 - half, 1), h, rw, 1 - half, left, own_part(h, 1 - half))
        send(("own_s",), h, rw, 0, sibling, own_part(h, 0, 2), n=2)

    def from_z(h, g, is_inner, halves=(0, 1)):
        zs = sources[g]
        r = rows_of(zs, y, c)
        target = at_rows(jnp.where(zs < z, lax.rem(z + 1, RING), ring(z, -1)), y, c)
        for half in halves:
            arrive(h, r, half)
            if is_inner:
                send(("z_z", g, half), h, r, half, target, cond=inner)
            send(("z_y", g, half, 0), h, r, half, right)
            send(("z_y", g, half, 1), h, r, half, left)
        if 1 in halves:
            send(("z_s", g), h, r, 0, sibling, n=2)

    def from_two(h, g, is_inner):
        for half in (0, 1):
            from_z(h, g, is_inner, (half,))
            from_z(h, g + 1, is_inner, (half,))

    def from_y(h, g, is_inner):
        r_left = rows_of(sources[g], ring(y, -1), c)
        r_right = rows_of(sources[g], ring(y, 1), c)
        arrive(h, r_left, 0)
        send(("y_y", g, 0), h, r_left, 0, right)
        arrive(h, r_right, 1)
        send(("y_y", g, 1), h, r_right, 1, left)
        arrive(h, r_left, 1)
        send(("y_s", g, 0), h, r_left, 0, sibling, n=2)
        arrive(h, r_right, 0)
        send(("y_s", g, 1), h, r_right, 0, sibling, n=2)

    def from_far(h, g, is_inner):
        r = rows_of(sources[g], ring(y, 2), c)
        for half in (0, 1):
            arrive(h, r, half)
        send(("f_s", g), h, r, 0, sibling, n=2)

    def from_sibling(h):
        for zs in range(RING):
            for ys in range(RING):
                arrive(h, rows_of(zs, ys, 1 - c), 0, 2)

    def local_part(h):
        copy = pltpu.make_async_copy(
            high.at[:, :, pl.ds(LANES * h, LANES)], gathered[h].at[pl.ds(rw * 4, 4)], local_sem.at[h]
        )
        copy.start()
        return copy

    def by_place(inner_steps, end_steps):
        for is_inner, steps in ((True, inner_steps), (False, end_steps)):

            @pl.when(inner if is_inner else jnp.logical_not(inner))
            def _(is_inner=is_inner, steps=steps):
                for step in steps:
                    step[0](*step[1:], is_inner)

    LOW_PARTS = 4

    def send_low_to(key, j, target, src, part):
        dst = low_buf.at[j, pl.ds(part * 256, 256)]
        if src is None:
            src = dst
        sem = send_low.at[slots.setdefault(("low", key), sum(k[0] == "low" for k in slots))]
        copy = remote(src, dst, sem, recv_low.at[j, part], target)
        copy.start()
        waits[("low", key)] = (0, None)

    def arrive_low(j, part):
        dst = low_buf.at[j, pl.ds(part * 256, 256)]
        remote(dst, dst, send_low.at[0], recv_low.at[j, part], sibling).wait_recv()

    j_across = (1 - zh) * RING + x

    def low_x(is_inner):
        for part in range(LOW_PARTS):
            for d in range(3):
                send_low_to(("x", d, part), jp, x_others[d], low.at[pl.ds(part * 256, 256)], part)

    def low_across(part, is_inner):
        send_low_to(("across", part), jp, across, low.at[pl.ds(part * 256, 256)], part)

    def low_onward(part, is_inner):
        arrive_low(j_across, part)
        for d in range(3):
            send_low_to(("onward", d, part), j_across, x_others[d], None, part)

    def low_finish():
        own_low.wait()
        for part in range(LOW_PARTS):
            for d in (1, 2, 3):
                arrive_low(zh * RING + ring(x, d), part)
            for d in (1, 2, 3):
                arrive_low((1 - zh) * RING + ring(x, d), part)

    def low_turn(j):
        low_t[pl.ds(j * BLK, BLK), :] = low_buf[j].T

    def apply_rows(h, q):
        def some(i, total):
            for k in range(4):
                b = q * 16 + i * 4 + k
                total = total + jnp.dot(d_buf[b], gathered[h][cols[rw * 64 + b]], preferred_element_type=jnp.float32)
            return total

        total = lax.fori_loop(0, 4, some, jnp.zeros((BLK, LANES), jnp.float32))
        applied[h, pl.ds(q * BLK, BLK), :] = total.astype(jnp.bfloat16)

    def tile_rows(h, j0, n):
        def one(j, _):
            part = jnp.dot(
                low_t[pl.ds(pl.multiple_of(j * BLK, BLK), BLK), :], applied[h], preferred_element_type=jnp.float32
            )
            tiles[h][pl.ds(2 * j, 2)] = part.reshape(2, 2, 64, LANES)
            return 0

        lax.fori_loop(j0, j0 + n, one, 0)

    def sum_copy(h, k, src, dst, target):
        return remote(src, dst, send_sum.at[h, k], recv_sum.at[h, k], target)

    def sum_sibling(h):
        copy = sum_copy(h, 0, tiles[h].at[:, 1 - c], sib_buf.at[h], sibling)
        copy.start()
        return copy

    def sum_y_start(h, sib_copy):
        sib_copy.wait()
        copies = []
        for d in (2, 1, 3):
            for zs in range(RING):
                p = zs * RING + ring(y, d)
                y_send[h, d, zs] = (tiles[h][p, c] + sib_buf[h, p]).astype(Y_TYPE)
            copy = sum_copy(h, d, y_send.at[h, d], y_recv.at[h, d], y_others[d - 1])
            copy.start()
            copies.append(copy)
        return copies

    def sum_z_start(h, y_copies):
        for copy in y_copies:
            copy.wait()

        def one(zs):
            p = zs * RING + y
            total = tiles[h][p, c] + sib_buf[h, p]
            for d in (1, 2, 3):
                total = total + y_recv[h, d, zs].astype(jnp.float32)
            return total

        copies = []
        for d in (3, 2, 1):
            z_send[h, d] = one(ring(z, d)).astype(Z_TYPE)
            copy = sum_copy(h, 3 + d, z_send.at[h, d], z_recv.at[h, d], z_others[d - 1])
            copy.start()
            copies.append(copy)
        return copies, one(z)

    def sum_end(h, copies, total):
        for copy in copies:
            copy.wait()
        for d in (1, 2, 3):
            total = total + z_recv[h, d].astype(jnp.float32)
        out[:, LANES * h : LANES * (h + 1)] = total

    by_place([(own_z, 0), (own_y, 0)], [(own_z, 0), (own_y, 0)])
    local_0 = local_part(0)
    own_low = pltpu.make_async_copy(low, low_buf.at[jp], local_sem.at[2])
    own_low.start()
    dip_copy = pltpu.make_async_copy(dip, d_buf, local_sem.at[3])
    dip_copy.start()
    low_x(None)
    local_1 = local_part(1)
    by_place(
        [(from_two, 0, 1), (from_y, 0, 0), (from_z, 0, 3), (low_across, 0), (low_across, 1), (from_y, 0, 1), (from_far, 0, 0),
         (from_y, 0, 2), (own_y, 1), (own_z, 1), (low_across, 2), (from_far, 0, 1), (from_y, 0, 3), (from_far, 0, 2), (from_two, 1, 1), (from_far, 0, 3)],
        [(from_z, 0, 1), (from_y, 0, 0), (from_y, 0, 1), (from_z, 0, 2), (from_far, 0, 0), (from_z, 0, 3), (low_across, 0), (low_across, 1),
         (from_y, 0, 2), (from_far, 0, 1), (own_y, 1), (own_z, 1), (low_across, 2), (from_y, 0, 3), (from_far, 0, 2), (from_z, 1, 1), (from_far, 0, 3)],
    )
    from_sibling(0)
    local_0.wait()
    dip_copy.wait()
    by_place([(from_y, 1, 0), (from_z, 1, 3), (low_across, 3)], [(from_y, 1, 0), (from_z, 1, 2), (low_across, 3)])
    apply_rows(0, 0)
    low_onward(0, None)
    low_onward(1, None)
    by_place([(from_y, 1, 1)], [(from_y, 1, 1)])
    apply_rows(0, 1)
    by_place([], [(from_z, 1, 3)])
    apply_rows(0, 2)
    by_place([(from_far, 1, 0)], [(from_far, 1, 0)])
    low_onward(2, None)
    apply_rows(0, 3)
    by_place([(from_y, 1, 2)], [(from_y, 1, 2)])
    low_onward(3, None)
    by_place([(from_far, 1, 1)], [(from_far, 1, 1)])
    by_place([(from_y, 1, 3)], [(from_y, 1, 3)])
    low_finish()
    for j in range(8):
        low_turn(j)
    by_place([(from_far, 1, 2)], [(from_far, 1, 2)])
    tile_rows(0, 0, 8)
    sib_copy = sum_sibling(0)
    by_place([(from_far, 1, 3)], [(from_far, 1, 3)])
    y_copies = sum_y_start(0, sib_copy)
    from_sibling(1)
    local_1.wait()
    apply_rows(1, 0)
    z_copies, mine = sum_z_start(0, y_copies)
    for q in range(1, 4):
        apply_rows(1, q)
    sum_end(0, z_copies, mine)
    tile_rows(1, 0, 8)
    sib_copy = sum_sibling(1)
    y_copies = sum_y_start(1, sib_copy)
    z_copies, mine = sum_z_start(1, y_copies)
    for (h, key), (n, cond) in waits.items():
        slot = slots[(h, key)]
        if h == "low":
            ref = low_buf.at[0, pl.ds(0, 256)]
            copy = remote(ref, ref, send_low.at[slot], recv_low.at[0, 0], sibling)
        else:
            ref = gathered[h].at[pl.ds(0, 2 * n)]
            copy = remote(ref, ref, send_g.at[h, slot], recv_g.at[h, 0, 0], sibling)
        if cond is None:
            copy.wait_send()
        else:
            pl.when(cond)(copy.wait_send)
    sum_end(1, z_copies, mine)


def shards(psi_low, psi_high, dip_blocks, block_cols):
    any_space = pl.BlockSpec(memory_space=pl.ANY)
    return pl.pallas_call(
        kernel,
        out_shape=jax.ShapeDtypeStruct((64, 256), jnp.float32),
        in_specs=[pl.BlockSpec(memory_space=pltpu.SMEM), any_space, any_space, any_space],
        out_specs=pl.BlockSpec(memory_space=pltpu.VMEM),
        scratch_shapes=[
            pltpu.VMEM((128, BLK, LANES), jnp.bfloat16),
            pltpu.VMEM((128, BLK, LANES), jnp.bfloat16),
            pltpu.VMEM((64, BLK, BLK), jnp.bfloat16),
            pltpu.VMEM((8, 1024, 256), jnp.bfloat16),
            pltpu.VMEM((2048, 1024), jnp.bfloat16),
            pltpu.VMEM((2, 1024, LANES), jnp.bfloat16),
            pltpu.VMEM((16, 2, 64, LANES), jnp.float32),
            pltpu.VMEM((16, 2, 64, LANES), jnp.float32),
            pltpu.VMEM((2, 16, 64, LANES), jnp.float32),
            pltpu.VMEM((2, 4, 4, 64, LANES), Y_TYPE),
            pltpu.VMEM((2, 4, 4, 64, LANES), Y_TYPE),
            pltpu.VMEM((2, 4, 64, LANES), Z_TYPE),
            pltpu.VMEM((2, 4, 64, LANES), Z_TYPE),
            pltpu.SemaphoreType.DMA((2, 32, 2)),
            pltpu.SemaphoreType.DMA((2, 72)),
            pltpu.SemaphoreType.DMA((8, 4)),
            pltpu.SemaphoreType.DMA((32,)),
            pltpu.SemaphoreType.DMA((2, 8)),
            pltpu.SemaphoreType.DMA((2, 8)),
            pltpu.SemaphoreType.DMA((4,)),
        ],
        compiler_params=pltpu.CompilerParams(
            collective_id=0, has_side_effects=True, vmem_limit_bytes=56 * 1024 * 1024
        ),
        cost_estimate=pl.CostEstimate(flops=3 * 2**30, bytes_accessed=10 * 2**20, transcendentals=0),
    )(block_cols, psi_low, psi_high.reshape(4, BLK, 256), dip_blocks)


def solution(mesh):
    placed = (P("rows", "jpair"), P("rows", "jpair"), P("rows", None, None), P())
    return jax.shard_map(
        shards, mesh=mesh, in_specs=placed, out_specs=P("rows", "jpair"), check_vma=False
    )
```

```python
import functools

import jax
import jax.numpy as jnp
from jax import lax
from jax.experimental import pallas as pl
from jax.experimental.pallas import tpu as pltpu
from jax.sharding import PartitionSpec as P

BLK = 256
LANES = 128
MESH = pl.DeviceIdType.MESH
RING = 4
GROUP = 4
Y_TYPE = jnp.bfloat16
Z_TYPE = jnp.bfloat16


def kernel(
    cols_all, low, high, dip, out,
    g_a, g_b, d_buf, low_buf, low_t, applied, tile_a, tile_b, sib_buf, y_send, y_recv, z_send, z_recv,
    recv_g, send_g, recv_low, send_low, recv_sum, send_sum, local_sem, cols,
):
    gathered = (g_a, g_b)
    tiles = (tile_a, tile_b)
    jp = lax.axis_index("jpair")
    rw = lax.axis_index("rows")
    x, zh = lax.rem(jp, RING), lax.div(jp, RING)
    c, y, z = lax.rem(rw, 2), lax.rem(lax.div(rw, 2), RING), lax.div(rw, 2 * RING)

    def rows_of(zs, ys, cs):
        return (zs * RING + ys) * 2 + cs

    def ring(v, step):
        return lax.rem(v + step + RING, RING)

    def at_rows(zs, ys, cs):
        return (jp, rows_of(zs, ys, cs))

    def at_jpair(zhs, xs):
        return (zhs * RING + xs, rw)

    right, left = at_rows(z, ring(y, 1), c), at_rows(z, ring(y, -1), c)
    sibling = at_rows(z, y, 1 - c)
    y_others = [at_rows(z, ring(y, d), c) for d in (1, 2, 3)]
    z_others = [at_rows(ring(z, d), y, c) for d in (1, 2, 3)]
    x_others = [at_jpair(zh, ring(x, d)) for d in (1, 2, 3)]
    across = at_jpair(1 - zh, x)

    barrier = pltpu.get_barrier_semaphore()
    partners = [sibling, across] + y_others + z_others + x_others
    for partner in partners:
        pl.semaphore_signal(barrier, inc=1, device_id=partner, device_id_type=MESH)
    pl.semaphore_wait(barrier, len(partners))

    waits = {}

    def remote(src, dst, send_sem, recv_sem, target):
        return pltpu.make_async_remote_copy(
            src_ref=src, dst_ref=dst, send_sem=send_sem, recv_sem=recv_sem,
            device_id=target, device_id_type=MESH,
        )

    inner = jnp.logical_and(z > 0, z < RING - 1)
    slots = {}

    def piece(h, r, half, n=1):
        return gathered[h].at[pl.ds(r * 4 + 2 * half, 2 * n)]

    def send(key, h, r, half, target, src=None, n=1, cond=None):
        dst = piece(h, r, half, n)
        sem = send_g.at[h, slots.setdefault((h, key), sum(k[0] == h for k in slots))]
        copy = remote(dst if src is None else src, dst, sem, recv_g.at[h, r, half], target)
        copy.start()
        waits[(h, key)] = (n, cond)

    def arrive(h, r, half, n=1):
        ref = piece(h, r, half, n)
        remote(ref, ref, send_g.at[h, 0], recv_g.at[h, r, half], sibling).wait_recv()

    def own_part(h, half, n=1):
        return high.at[pl.ds(2 * half, 2 * n), :, pl.ds(LANES * h, LANES)]

    onward = at_rows(jnp.where(z == RING - 1, z - 1, z + 1), y, c)
    downward = at_rows(ring(z, -1), y, c)
    sources = [z, z + 1 - 2 * lax.rem(z, 2), jnp.where(z < 2, 2, 1), jnp.where(z < 2, 3, 0)]

    def own_z(h, is_inner):
        for half in (0, 1):
            send(("own_z", half, 0), h, rw, half, onward, own_part(h, half))
            if is_inner:
                send(("own_z", half, 1), h, rw, half, downward, own_part(h, half), cond=inner)

    def own_y(h, is_inner):
        for half in (0, 1):
            send(("own_y", half, 0), h, rw, half, right, own_part(h, half))
            send(("own_y", 1 - half, 1), h, rw, 1 - half, left, own_part(h, 1 - half))
        send(("own_s",), h, rw, 0, sibling, own_part(h, 0, 2), n=2)

    def from_z(h, g, is_inner, halves=(0, 1)):
        zs = sources[g]
        r = rows_of(zs, y, c)
        target = at_rows(jnp.where(zs < z, lax.rem(z + 1, RING), ring(z, -1)), y, c)
        for half in halves:
            arrive(h, r, half)
            if is_inner:
                send(("z_z", g, half), h, r, half, target, cond=inner)
            send(("z_y", g, half, 0), h, r, half, right)
            send(("z_y", g, half, 1), h, r, half, left)
        if 1 in halves:
            send(("z_s", g), h, r, 0, sibling, n=2)

    def from_two(h, g, is_inner):
        for half in (0, 1):
            from_z(h, g, is_inner, (half,))
            from_z(h, g + 1, is_inner, (half,))

    def from_y(h, g, is_inner):
        r_left = rows_of(sources[g], ring(y, -1), c)
        r_right = rows_of(sources[g], ring(y, 1), c)
        arrive(h, r_left, 0)
        send(("y_y", g, 0), h, r_left, 0, right)
        arrive(h, r_right, 1)
        send(("y_y", g, 1), h, r_right, 1, left)
        arrive(h, r_left, 1)
        send(("y_s", g, 0), h, r_left, 0, sibling, n=2)
        arrive(h, r_right, 0)
        send(("y_s", g, 1), h, r_right, 0, sibling, n=2)

    def from_far(h, g, is_inner):
        r = rows_of(sources[g], ring(y, 2), c)
        for half in (0, 1):
            arrive(h, r, half)
        send(("f_s", g), h, r, 0, sibling, n=2)

    def from_sibling(h):
        for zs in range(RING):
            for ys in range(RING):
                arrive(h, rows_of(zs, ys, 1 - c), 0, 2)

    def local_part(h):
        copy = pltpu.make_async_copy(
            high.at[:, :, pl.ds(LANES * h, LANES)], gathered[h].at[pl.ds(rw * 4, 4)], local_sem.at[h]
        )
        copy.start()
        return copy

    def by_place(inner_steps, end_steps):
        for is_inner, steps in ((True, inner_steps), (False, end_steps)):

            @pl.when(inner if is_inner else jnp.logical_not(inner))
            def _(is_inner=is_inner, steps=steps):
                for step in steps:
                    step[0](*step[1:], is_inner)

    LOW_PARTS = 4

    def send_low_to(key, j, target, src, part):
        dst = low_buf.at[j, pl.ds(part * 256, 256)]
        if src is None:
            src = dst
        sem = send_low.at[slots.setdefault(("low", key), sum(k[0] == "low" for k in slots))]
        copy = remote(src, dst, sem, recv_low.at[j, part], target)
        copy.start()
        waits[("low", key)] = (0, None)

    def arrive_low(j, part):
        dst = low_buf.at[j, pl.ds(part * 256, 256)]
        remote(dst, dst, send_low.at[0], recv_low.at[j, part], sibling).wait_recv()

    j_across = (1 - zh) * RING + x

    def low_x(is_inner):
        for part in range(LOW_PARTS):
            for d in range(3):
                send_low_to(("x", d, part), jp, x_others[d], low.at[pl.ds(part * 256, 256)], part)

    def low_across(part, is_inner):
        send_low_to(("across", part), jp, across, low.at[pl.ds(part * 256, 256)], part)

    def low_onward(part, is_inner):
        arrive_low(j_across, part)
        for d in range(3):
            send_low_to(("onward", d, part), j_across, x_others[d], None, part)

    def low_finish():
        own_low.wait()
        for part in range(LOW_PARTS):
            for d in (1, 2, 3):
                arrive_low(zh * RING + ring(x, d), part)
            for d in (1, 2, 3):
                arrive_low((1 - zh) * RING + ring(x, d), part)

    def low_turn(j):
        low_t[pl.ds(j * BLK, BLK), :] = low_buf[j].T

    def apply_rows(h, q):
        def some(i, total):
            b = q * 16 + i * GROUP
            lhs = jnp.concatenate([d_buf[b + k] for k in range(GROUP)], axis=1)
            rhs = jnp.concatenate([gathered[h][cols[rw * 64 + b + k]] for k in range(GROUP)], axis=0)
            return total + jnp.dot(lhs, rhs, preferred_element_type=jnp.float32)

        total = lax.fori_loop(0, 16 // GROUP, some, jnp.zeros((BLK, LANES), jnp.float32))
        applied[h, pl.ds(q * BLK, BLK), :] = total.astype(jnp.bfloat16)

    quarters = [ring(z, d) for d in (2, 3, 1, 0)]
    quarter_shift = (2, 3, 1)

    def sum_copy(h, k, src, dst, target):
        return remote(src, dst, send_sum.at[h, k], recv_sum.at[h, k], target)

    def sib_copy(h, i):
        part = pl.ds(4 * quarters[i], 4)
        return sum_copy(h, i, tiles[h].at[part, 1 - c], sib_buf.at[h, part], sibling)

    def y_copy(h, i, d):
        return sum_copy(h, 3 + 3 * i + d, y_send.at[h, d, i], y_recv.at[h, d, i], y_others[d - 1])

    def z_copy(h, i):
        return sum_copy(h, 16 + i, z_send.at[h, i], z_recv.at[h, i], z_others[quarter_shift[i] - 1])

    def tile_quarter(h, i):
        rows = pl.ds(pl.multiple_of(quarters[i] * 512, 512), 512)
        part = jnp.dot(low_t[rows, :], applied[h], preferred_element_type=jnp.float32)
        tiles[h][pl.ds(4 * quarters[i], 4)] = part.reshape(4, 2, 64, LANES)
        sib_copy(h, i).start()

    def y_quarter(h, i):
        sib_copy(h, i).wait()
        for d in (2, 1, 3):
            p = quarters[i] * 4 + ring(y, d)
            y_send[h, d, i] = (tiles[h][p, c] + sib_buf[h, p]).astype(Y_TYPE)
            y_copy(h, i, d).start()

    def z_quarter(h, i):
        for d in (1, 2, 3):
            y_copy(h, i, d).wait()
        p = quarters[i] * 4 + y
        total = tiles[h][p, c] + sib_buf[h, p]
        for d in (1, 2, 3):
            total = total + y_recv[h, d, i].astype(jnp.float32)
        if i == 3:
            return total
        z_send[h, i] = total.astype(Z_TYPE)
        z_copy(h, i).start()

    def sum_end(h, total):
        for i in range(3):
            z_copy(h, i).wait()
            total = total + z_recv[h, i].astype(jnp.float32)
        out[:, LANES * h : LANES * (h + 1)] = total

    by_place([(own_z, 0), (own_y, 0)], [(own_z, 0), (own_y, 0)])
    local_0 = local_part(0)
    low_x(None)
    own_low = pltpu.make_async_copy(low, low_buf.at[jp], local_sem.at[2])
    own_low.start()
    dip_copy = pltpu.make_async_copy(dip, d_buf, local_sem.at[3])
    dip_copy.start()
    cols_copy = pltpu.make_async_copy(cols_all, cols, local_sem.at[4])
    cols_copy.start()
    local_1 = local_part(1)
    by_place(
        [(from_two, 0, 1), (low_across, 0), (from_y, 0, 0), (from_z, 0, 3), (low_across, 1), (low_across, 2), (from_y, 0, 1), (from_far, 0, 0),
         (from_y, 0, 2), (own_y, 1), (own_z, 1), (low_onward, 0), (from_far, 0, 1), (from_y, 0, 3), (low_onward, 1), (from_far, 0, 2), (from_two, 1, 1), (from_far, 0, 3)],
        [(from_z, 0, 1), (from_y, 0, 0), (from_y, 0, 1), (from_z, 0, 2), (low_across, 0), (from_far, 0, 0), (from_z, 0, 3), (low_across, 1), (low_across, 2),
         (from_y, 0, 2), (from_far, 0, 1), (own_y, 1), (own_z, 1), (low_onward, 0), (from_y, 0, 3), (low_onward, 1), (from_far, 0, 2), (from_z, 1, 1), (from_far, 0, 3)],
    )
    from_sibling(0)
    local_0.wait()
    dip_copy.wait()
    cols_copy.wait()
    by_place([(from_y, 1, 0), (low_across, 3), (low_onward, 2), (from_z, 1, 3)], [(from_y, 1, 0), (low_onward, 2), (from_z, 1, 2), (low_across, 3)])
    apply_rows(0, 0)
    apply_rows(0, 1)
    by_place([(from_y, 1, 1)], [(from_y, 1, 1)])
    apply_rows(0, 2)
    apply_rows(0, 3)
    by_place([(from_far, 1, 0)], [(from_z, 1, 3), (from_far, 1, 0)])
    low_onward(3, None)
    by_place([(from_y, 1, 2)], [(from_y, 1, 2)])
    low_finish()
    for j in range(8):
        low_turn(j)
    for i in range(4):
        tile_quarter(0, i)
    by_place([(from_far, 1, 1)], [(from_far, 1, 1)])
    for i in range(4):
        y_quarter(0, i)
    by_place([(from_y, 1, 3)], [(from_y, 1, 3)])
    by_place([(from_far, 1, 2)], [(from_far, 1, 2)])
    mine_0 = [z_quarter(0, i) for i in range(4)][3]
    by_place([(from_far, 1, 3)], [(from_far, 1, 3)])
    from_sibling(1)
    local_1.wait()
    for q in range(4):
        apply_rows(1, q)
    tile_quarter(1, 0)
    tile_quarter(1, 1)
    y_quarter(1, 0)
    tile_quarter(1, 2)
    y_quarter(1, 1)
    tile_quarter(1, 3)
    y_quarter(1, 2)
    y_quarter(1, 3)
    sum_end(0, mine_0)
    z_quarter(1, 0)
    z_quarter(1, 1)
    z_quarter(1, 2)
    mine_1 = z_quarter(1, 3)
    for (h, key), (n, cond) in waits.items():
        slot = slots[(h, key)]
        if h == "low":
            ref = low_buf.at[0, pl.ds(0, 256)]
            copy = remote(ref, ref, send_low.at[slot], recv_low.at[0, 0], sibling)
        else:
            ref = gathered[h].at[pl.ds(0, 2 * n)]
            copy = remote(ref, ref, send_g.at[h, slot], recv_g.at[h, 0, 0], sibling)
        if cond is None:
            copy.wait_send()
        else:
            pl.when(cond)(copy.wait_send)
    sum_end(1, mine_1)


def shards(psi_low, psi_high, dip_blocks, block_cols):
    any_space = pl.BlockSpec(memory_space=pl.ANY)
    return pl.pallas_call(
        kernel,
        out_shape=jax.ShapeDtypeStruct((64, 256), jnp.float32),
        in_specs=[any_space] * 4,
        out_specs=pl.BlockSpec(memory_space=pltpu.VMEM),
        scratch_shapes=[
            pltpu.VMEM((128, BLK, LANES), jnp.bfloat16),
            pltpu.VMEM((128, BLK, LANES), jnp.bfloat16),
            pltpu.VMEM((64, BLK, BLK), jnp.bfloat16),
            pltpu.VMEM((8, 1024, 256), jnp.bfloat16),
            pltpu.VMEM((2048, 1024), jnp.bfloat16),
            pltpu.VMEM((2, 1024, LANES), jnp.bfloat16),
            pltpu.VMEM((16, 2, 64, LANES), jnp.float32),
            pltpu.VMEM((16, 2, 64, LANES), jnp.float32),
            pltpu.VMEM((2, 16, 64, LANES), jnp.float32),
            pltpu.VMEM((2, 4, 4, 64, LANES), Y_TYPE),
            pltpu.VMEM((2, 4, 4, 64, LANES), Y_TYPE),
            pltpu.VMEM((2, 4, 64, LANES), Z_TYPE),
            pltpu.VMEM((2, 4, 64, LANES), Z_TYPE),
            pltpu.SemaphoreType.DMA((2, 32, 2)),
            pltpu.SemaphoreType.DMA((2, 72)),
            pltpu.SemaphoreType.DMA((8, 4)),
            pltpu.SemaphoreType.DMA((32,)),
            pltpu.SemaphoreType.DMA((2, 20)),
            pltpu.SemaphoreType.DMA((2, 20)),
            pltpu.SemaphoreType.DMA((5,)),
            pltpu.SMEM((2048,), jnp.int32),
        ],
        compiler_params=pltpu.CompilerParams(
            collective_id=0, has_side_effects=True, vmem_limit_bytes=56 * 1024 * 1024
        ),
        cost_estimate=pl.CostEstimate(flops=3 * 2**30, bytes_accessed=10 * 2**20, transcendentals=0),
    )(block_cols, psi_low, psi_high.reshape(4, BLK, 256), dip_blocks)


def solution(mesh):
    placed = (P("rows", "jpair"), P("rows", "jpair"), P("rows", None, None), P())
    return jax.shard_map(
        shards, mesh=mesh, in_specs=placed, out_specs=P("rows", "jpair"), check_vma=False
    )
```

```python
import functools

import jax
import jax.numpy as jnp
from jax import lax
from jax.experimental import pallas as pl
from jax.experimental.pallas import tpu as pltpu
from jax.sharding import PartitionSpec as P

BLK = 256
LANES = 128
MESH = pl.DeviceIdType.MESH
RING = 4
GROUP = 4
LATE = 16
Y_TYPE = jnp.bfloat16
Z_TYPE = jnp.bfloat16


def kernel(
    cols_all, low, high, dip, out,
    g_a, g_b, d_buf, low_buf, low_t, applied, tile_a, tile_b, sib_buf, y_send, y_recv, z_send, z_recv,
    recv_g, send_g, recv_low, send_low, recv_sum, send_sum, local_sem, cols,
    g_late, early, late_parts, late_list,
):
    gathered = (g_a, g_b)
    tiles = (tile_a, tile_b)
    jp = lax.axis_index("jpair")
    rw = lax.axis_index("rows")
    x, zh = lax.rem(jp, RING), lax.div(jp, RING)
    c, y, z = lax.rem(rw, 2), lax.rem(lax.div(rw, 2), RING), lax.div(rw, 2 * RING)

    def rows_of(zs, ys, cs):
        return (zs * RING + ys) * 2 + cs

    def ring(v, step):
        return lax.rem(v + step + RING, RING)

    def at_rows(zs, ys, cs):
        return (jp, rows_of(zs, ys, cs))

    def at_jpair(zhs, xs):
        return (zhs * RING + xs, rw)

    right, left = at_rows(z, ring(y, 1), c), at_rows(z, ring(y, -1), c)
    sibling = at_rows(z, y, 1 - c)
    y_others = [at_rows(z, ring(y, d), c) for d in (1, 2, 3)]
    z_others = [at_rows(ring(z, d), y, c) for d in (1, 2, 3)]
    x_others = [at_jpair(zh, ring(x, d)) for d in (1, 2, 3)]
    across = at_jpair(1 - zh, x)

    barrier = pltpu.get_barrier_semaphore()
    partners = [y_others[0], y_others[2], z_others[0], z_others[2], sibling, y_others[1], z_others[1]] + x_others + [across]
    for partner in partners:
        pl.semaphore_signal(barrier, inc=1, device_id=partner, device_id_type=MESH)
    pl.semaphore_wait(barrier, len(partners))

    waits = {}

    def remote(src, dst, send_sem, recv_sem, target):
        return pltpu.make_async_remote_copy(
            src_ref=src, dst_ref=dst, send_sem=send_sem, recv_sem=recv_sem,
            device_id=target, device_id_type=MESH,
        )

    inner = jnp.logical_and(z > 0, z < RING - 1)
    slots = {}

    def piece(h, r, half, n=1):
        return gathered[h].at[pl.ds(r * 4 + 2 * half, 2 * n)]

    def is_late(h, g):
        return h == 1 and g >= 2

    def late_piece(g, core, half, n=1):
        return g_late.at[pl.ds(((g - 2) * 2 + core) * 4 + 2 * half, 2 * n)]

    def send(key, h, r, half, target, src=None, n=1, cond=None, dst=None):
        dst = piece(h, r, half, n) if dst is None else dst
        sem = send_g.at[h, slots.setdefault((h, key), sum(k[0] == h for k in slots))]
        copy = remote(dst if src is None else src, dst, sem, recv_g.at[h, r, half], target)
        copy.start()
        waits[(h, key)] = (int(2 * n), cond)

    def arrive(h, r, half, n=1, ref=None):
        ref = piece(h, r, half, n) if ref is None else ref
        remote(ref, ref, send_g.at[h, 0], recv_g.at[h, r, half], sibling).wait_recv()

    def own_part(h, half, n=1):
        return high.at[pl.ds(2 * half, 2 * n), :, pl.ds(LANES * h, LANES)]

    onward = at_rows(jnp.where(z == RING - 1, z - 1, z + 1), y, c)
    downward = at_rows(ring(z, -1), y, c)
    sources = [z, z + 1 - 2 * lax.rem(z, 2), jnp.where(z < 2, 2, 1), jnp.where(z < 2, 3, 0)]

    def own_z(h, is_inner):
        for half in (0, 1):
            send(("own_z", half, 0), h, rw, half, onward, own_part(h, half))
            if is_inner:
                send(("own_z", half, 1), h, rw, half, downward, own_part(h, half), cond=inner)

    def own_y(h, is_inner):
        for half in (0, 1):
            send(("own_y", half, 0), h, rw, half, right, own_part(h, half))
            send(("own_y", 1 - half, 1), h, rw, 1 - half, left, own_part(h, 1 - half))
        send(("own_s",), h, rw, 0, sibling, own_part(h, 0, 2), n=2)

    def from_z(h, g, is_inner, halves=(0, 1)):
        zs = sources[g]
        r = rows_of(zs, y, c)
        target = at_rows(jnp.where(zs < z, lax.rem(z + 1, RING), ring(z, -1)), y, c)
        for half in halves:
            arrive(h, r, half)
            if is_inner:
                send(("z_z", g, half), h, r, half, target, cond=inner)
            send(("z_y", g, half, 0), h, r, half, right)
            send(("z_y", g, half, 1), h, r, half, left)
        if 1 in halves:
            send(("z_s", g), h, r, 0, sibling, n=2)

    def from_two(h, g, is_inner):
        for half in (0, 1):
            from_z(h, g, is_inner, (half,))
            from_z(h, g + 1, is_inner, (half,))

    def from_y(h, g, is_inner):
        r_left = rows_of(sources[g], ring(y, -1), c)
        r_right = rows_of(sources[g], ring(y, 1), c)
        arrive(h, r_left, 0)
        forward(("y_y", g, 0), h, g, r_left, 0, right)
        arrive(h, r_right, 1)
        forward(("y_y", g, 1), h, g, r_right, 1, left)
        arrive(h, r_left, 1)
        send(("y_s", g, 0), h, r_left, 0, sibling, n=2)
        arrive(h, r_right, 0)
        send(("y_s", g, 1), h, r_right, 0, sibling, n=2)

    def by_z(h, g):
        return g == 1 and False

    partner = at_rows(z + 1 - 2 * lax.rem(z, 2), y, c)

    def part_of(h, r, k, n):
        return gathered[h].at[pl.ds(r * 4 + k, n)]

    def forward(key, h, g, r, half, target):
        src = piece(h, r, half) if not by_z(h, g) else part_of(h, r, 3 * half, 1)
        dst = late_piece(g, c, half) if is_late(h, g) else src
        send(key, h, r, half, target, src=src, dst=dst, n=0.5 if by_z(h, g) else 1)

    def from_far(h, g, is_inner):
        r = rows_of(sources[g], ring(y, 2), c)
        for half in (0, 1):
            ref = late_piece(g, c, half) if is_late(h, g) else None
            arrive(h, r, half, ref=part_of(h, r, 3 * half, 1) if by_z(h, g) else ref)
        middle = part_of(h, r, 1, 2)
        if g == 0 and by_z(h, 1):
            send(("f_z",), h, r, 2, partner, src=middle, dst=middle)
        if by_z(h, g):
            arrive(h, r, 2, ref=middle)
        whole = late_piece(g, c, 0, 2) if is_late(h, g) else None
        send(("f_s", g), h, r, 0, sibling, n=2, src=whole, dst=whole)

    def from_sibling(h, late):
        for g in range(RING):
            for d in range(RING):
                if late != (is_late(h, g) and d == 2):
                    continue
                ref = late_piece(g, 1 - c, 0, 2) if late else None
                arrive(h, rows_of(sources[g], ring(y, d), 1 - c), 0, 2, ref)

    def local_part(h):
        copy = pltpu.make_async_copy(
            high.at[:, :, pl.ds(LANES * h, LANES)], gathered[h].at[pl.ds(rw * 4, 4)], local_sem.at[h]
        )
        copy.start()
        return copy

    def by_place(inner_steps, end_steps):
        for is_inner, steps in ((True, inner_steps), (False, end_steps)):

            @pl.when(inner if is_inner else jnp.logical_not(inner))
            def _(is_inner=is_inner, steps=steps):
                for step in steps:
                    step[0](*step[1:], is_inner)

    LOW_PARTS = 4

    def send_low_to(key, j, target, src, part):
        dst = low_buf.at[j, pl.ds(part * 256, 256)]
        if src is None:
            src = dst
        sem = send_low.at[slots.setdefault(("low", key), sum(k[0] == "low" for k in slots))]
        copy = remote(src, dst, sem, recv_low.at[j, part], target)
        copy.start()
        waits[("low", key)] = (0, None)

    def arrive_low(j, part):
        dst = low_buf.at[j, pl.ds(part * 256, 256)]
        remote(dst, dst, send_low.at[0], recv_low.at[j, part], sibling).wait_recv()

    j_across = (1 - zh) * RING + x

    def low_x(is_inner):
        for part in range(LOW_PARTS):
            for d in range(3):
                send_low_to(("x", d, part), jp, x_others[d], low.at[pl.ds(part * 256, 256)], part)

    def low_across(part, is_inner):
        send_low_to(("across", part), jp, across, low.at[pl.ds(part * 256, 256)], part)

    def low_onward(part, is_inner):
        arrive_low(j_across, part)
        for d in range(3):
            send_low_to(("onward", d, part), j_across, x_others[d], None, part)

    def low_arrive(zhs):
        for part in range(LOW_PARTS):
            for d in (1, 2, 3):
                arrive_low(zhs * RING + ring(x, d), part)

    def low_turn(zhs):
        for i in range(RING):
            j = zhs * RING + i
            low_t[pl.ds(pl.multiple_of(j * BLK, BLK), BLK), :] = low_buf[j].T

    def place_of(b):
        col = cols[rw * 64 + b]
        chip = lax.shift_right_logical(col, 3)
        late_2 = chip == sources[2] * RING + ring(y, 2)
        late_3 = chip == sources[3] * RING + ring(y, 2)
        return col, jnp.logical_or(late_2, late_3), jnp.bitwise_and(col, 7) + 8 * late_3.astype(jnp.int32)

    def block_of(h, b):
        col, late, _ = place_of(b)
        return gathered[h][col if h == 0 else jnp.where(late, 128, col)]

    def apply_rows(h, q):
        def some(i, total):
            b = q * 16 + i * GROUP
            lhs = jnp.concatenate([d_buf[b + k] for k in range(GROUP)], axis=1)
            rhs = jnp.concatenate([block_of(h, b + k) for k in range(GROUP)], axis=0)
            return total + jnp.dot(lhs, rhs, preferred_element_type=jnp.float32)

        total = lax.fori_loop(0, 16 // GROUP, some, jnp.zeros((BLK, LANES), jnp.float32))
        if h == 0:
            applied[h, pl.ds(q * BLK, BLK), :] = total.astype(jnp.bfloat16)
        else:
            early[pl.ds(q * BLK, BLK), :] = total

    def list_late():
        def one(b, carry):
            count, found = carry[0], carry[1:]
            _, late, _ = place_of(b)
            found = tuple(jnp.where(jnp.logical_and(late, count == i), b, f) for i, f in enumerate(found))
            return (count + late.astype(jnp.int32),) + found

        carry = (jnp.int32(0),) + (jnp.int32(0),) * LATE
        for q in range(4):
            late_list[LATE + q] = jnp.minimum(carry[0], LATE)
            carry = lax.fori_loop(16 * q, 16 * q + 16, one, carry)
        late_list[LATE + 4] = jnp.minimum(carry[0], LATE)
        for i in range(LATE):
            late_list[i] = carry[1 + i]

    def apply_late():
        late_parts[0] = jnp.zeros((BLK, LANES), jnp.float32)

        def one(i, total):
            for k in range(4):
                b = jnp.bitwise_and(late_list[4 * i + k], 63)
                _, _, at = place_of(b)
                total = total + jnp.dot(d_buf[b], g_late[at], preferred_element_type=jnp.float32)
                late_parts[4 * i + k + 1] = total
            return total

        lax.fori_loop(0, LATE // 4, one, jnp.zeros((BLK, LANES), jnp.float32))
        for q in range(4):
            here = pl.ds(q * BLK, BLK)
            first, last = (jnp.clip(late_list[LATE + q + k], 0, LATE) for k in (0, 1))
            total = early[here, :] + (late_parts[last] - late_parts[first])
            applied[1, here, :] = total.astype(jnp.bfloat16)

    quarters = [3 - z, jnp.where(z < 2, z + 2, z - 2), z + 1 - 2 * lax.rem(z, 2), z]

    def sum_copy(h, k, src, dst, target):
        return remote(src, dst, send_sum.at[h, k], recv_sum.at[h, k], target)

    def sib_copy(h, i):
        part = pl.ds(4 * quarters[i], 4)
        return sum_copy(h, i, tiles[h].at[part, 1 - c], sib_buf.at[h, part], sibling)

    def y_copy(h, i, d):
        return sum_copy(h, 3 + 3 * i + d, y_send.at[h, d, i], y_recv.at[h, d, i], y_others[d - 1])

    def z_copy(h, i):
        return sum_copy(h, 16 + i, z_send.at[h, i], z_recv.at[h, i], at_rows(quarters[i], y, c))

    def tile_quarter(h, i, start=True):
        rows = pl.ds(pl.multiple_of(quarters[i] * 512, 512), 512)
        part = jnp.dot(low_t[rows, :], applied[h], preferred_element_type=jnp.float32)
        tiles[h][pl.ds(4 * quarters[i], 4)] = part.reshape(4, 2, 64, LANES)
        if start:
            sib_copy(h, i).start()

    def y_quarter(h, i):
        sib_copy(h, i).wait()
        for d in (2, 1, 3):
            p = quarters[i] * 4 + ring(y, d)
            y_send[h, d, i] = (tiles[h][p, c] + sib_buf[h, p]).astype(Y_TYPE)
            y_copy(h, i, d).start()

    def z_quarter(h, i):
        if h == 1:
            for d in (1, 2, 3):
                y_copy(h, i, d).wait()
        p = quarters[i] * 4 + y
        total = tiles[h][p, c] + sib_buf[h, p]
        for d in (1, 2, 3):
            total = total + y_recv[h, d, i].astype(jnp.float32)
        if i == 3:
            return total
        z_send[h, i] = total.astype(Z_TYPE)
        z_copy(h, i).start()

    def sib_whole():
        return sum_copy(0, 0, tiles[0].at[:, 1 - c], sib_buf.at[0], sibling)

    def y_whole(d):
        return sum_copy(0, 3 + d, y_send.at[0, d], y_recv.at[0, d], y_others[d - 1])

    def tile_whole():
        for i in range(4):
            tile_quarter(0, i, False)
        sib_whole().start()

    def y_whole_fill():
        sib_whole().wait()
        for d in (2, 1, 3):
            for i in range(4):
                p = quarters[i] * 4 + ring(y, d)
                y_send[0, d, i] = (tiles[0][p, c] + sib_buf[0, p]).astype(Y_TYPE)

    def y_whole_start():
        for d in (2, 1, 3):
            y_whole(d).start()

    def y_whole_wait():
        for d in (2, 1, 3):
            y_whole(d).wait()

    def sum_end(h, total):
        for i in range(3):
            z_copy(h, i).wait()
            total = total + z_recv[h, i].astype(jnp.float32)
        out[:, LANES * h : LANES * (h + 1)] = total

    cols_copy = pltpu.make_async_copy(cols_all, cols, local_sem.at[4])
    cols_copy.start()
    by_place([(own_z, 0), (own_y, 0)], [(own_z, 0), (own_y, 0)])
    local_0 = local_part(0)
    low_x(None)
    own_low = pltpu.make_async_copy(low, low_buf.at[jp], local_sem.at[2])
    own_low.start()
    dip_copy = pltpu.make_async_copy(dip, d_buf, local_sem.at[3])
    dip_copy.start()
    local_1 = local_part(1)
    gathered[1][128] = jnp.zeros((BLK, LANES), jnp.bfloat16)
    cols_copy.wait()
    list_late()
    by_place(
        [(from_two, 0, 1), (low_across, 0), (from_y, 0, 0), (from_z, 0, 3), (low_across, 1), (low_across, 2), (from_y, 0, 1), (from_far, 0, 0),
         (from_y, 0, 2), (own_y, 1), (own_z, 1), (low_across, 3), (low_onward, 0), (from_far, 0, 1)],
        [(from_z, 0, 1), (from_y, 0, 0), (from_y, 0, 1), (from_z, 0, 2), (low_across, 0), (from_far, 0, 0), (from_z, 0, 3), (low_across, 1), (low_across, 2),
         (from_y, 0, 2), (from_far, 0, 1), (own_y, 1), (own_z, 1), (low_across, 3), (low_onward, 0)],
    )
    own_low.wait()
    low_arrive(zh)
    low_turn(zh)
    by_place(
        [(from_y, 0, 3), (low_onward, 1), (from_far, 0, 2), (from_two, 1, 1), (from_far, 0, 3)],
        [(from_y, 0, 3), (low_onward, 1), (from_far, 0, 2), (from_z, 1, 1), (from_far, 0, 3)],
    )
    from_sibling(0, False)
    local_0.wait()
    dip_copy.wait()
    by_place([(from_y, 1, 0), (low_onward, 2), (from_z, 1, 3)], [(from_y, 1, 0), (low_onward, 2), (from_z, 1, 2)])
    apply_rows(0, 0)
    apply_rows(0, 1)
    by_place([(from_y, 1, 1)], [(from_y, 1, 1)])
    apply_rows(0, 2)
    apply_rows(0, 3)
    by_place([(from_far, 1, 0)], [(from_z, 1, 3), (from_far, 1, 0)])
    low_onward(3, None)
    by_place([(from_y, 1, 2)], [(from_y, 1, 2)])
    by_place([(from_far, 1, 1)], [(from_far, 1, 1)])
    low_arrive(1 - zh)
    low_turn(1 - zh)
    by_place([(from_y, 1, 3)], [(from_y, 1, 3)])
    tile_whole()
    y_whole_fill()
    y_whole_start()
    from_sibling(1, False)
    local_1.wait()
    apply_rows(1, 0)
    apply_rows(1, 1)
    by_place([(from_far, 1, 2)], [(from_far, 1, 2)])
    apply_rows(1, 2)
    apply_rows(1, 3)
    by_place([(from_far, 1, 3)], [(from_far, 1, 3)])
    from_sibling(1, True)
    apply_late()
    tile_quarter(1, 0)
    tile_quarter(1, 1)
    tile_quarter(1, 2)
    y_quarter(1, 0)
    y_quarter(1, 1)
    y_quarter(1, 2)
    tile_quarter(1, 3)
    y_quarter(1, 3)
    y_whole_wait()
    mine_0 = [z_quarter(0, i) for i in range(4)][3]
    z_quarter(1, 0)
    z_quarter(1, 1)
    z_quarter(1, 2)
    mine_1 = z_quarter(1, 3)
    sum_end(0, mine_0)
    for (h, key), (n, cond) in waits.items():
        slot = slots[(h, key)]
        if h == "low":
            ref = low_buf.at[0, pl.ds(0, 256)]
            copy = remote(ref, ref, send_low.at[slot], recv_low.at[0, 0], sibling)
        else:
            ref = gathered[h].at[pl.ds(0, n)]
            copy = remote(ref, ref, send_g.at[h, slot], recv_g.at[h, 0, 0], sibling)
        if cond is None:
            copy.wait_send()
        else:
            pl.when(cond)(copy.wait_send)
    sum_end(1, mine_1)


def shards(psi_low, psi_high, dip_blocks, block_cols):
    any_space = pl.BlockSpec(memory_space=pl.ANY)
    return pl.pallas_call(
        kernel,
        out_shape=jax.ShapeDtypeStruct((64, 256), jnp.float32),
        in_specs=[any_space] * 4,
        out_specs=pl.BlockSpec(memory_space=pltpu.VMEM),
        scratch_shapes=[
            pltpu.VMEM((128, BLK, LANES), jnp.bfloat16),
            pltpu.VMEM((129, BLK, LANES), jnp.bfloat16),
            pltpu.VMEM((64, BLK, BLK), jnp.bfloat16),
            pltpu.VMEM((8, 1024, 256), jnp.bfloat16),
            pltpu.VMEM((2048, 1024), jnp.bfloat16),
            pltpu.VMEM((2, 1024, LANES), jnp.bfloat16),
            pltpu.VMEM((16, 2, 64, LANES), jnp.float32),
            pltpu.VMEM((16, 2, 64, LANES), jnp.float32),
            pltpu.VMEM((2, 16, 64, LANES), jnp.float32),
            pltpu.VMEM((2, 4, 4, 64, LANES), Y_TYPE),
            pltpu.VMEM((2, 4, 4, 64, LANES), Y_TYPE),
            pltpu.VMEM((2, 4, 64, LANES), Z_TYPE),
            pltpu.VMEM((2, 4, 64, LANES), Z_TYPE),
            pltpu.SemaphoreType.DMA((2, 32, 3)),
            pltpu.SemaphoreType.DMA((2, 72)),
            pltpu.SemaphoreType.DMA((8, 4)),
            pltpu.SemaphoreType.DMA((32,)),
            pltpu.SemaphoreType.DMA((2, 20)),
            pltpu.SemaphoreType.DMA((2, 20)),
            pltpu.SemaphoreType.DMA((5,)),
            pltpu.SMEM((2048,), jnp.int32),
            pltpu.VMEM((LATE, BLK, LANES), jnp.bfloat16),
            pltpu.VMEM((1024, LANES), jnp.float32),
            pltpu.VMEM((LATE + 1, BLK, LANES), jnp.float32),
            pltpu.SMEM((LATE + 5,), jnp.int32),
        ],
        compiler_params=pltpu.CompilerParams(
            collective_id=0, has_side_effects=True, vmem_limit_bytes=56 * 1024 * 1024
        ),
        cost_estimate=pl.CostEstimate(flops=3 * 2**30, bytes_accessed=10 * 2**20, transcendentals=0),
    )(block_cols, psi_low, psi_high.reshape(4, BLK, 256), dip_blocks)


def solution(mesh):
    placed = (P("rows", "jpair"), P("rows", "jpair"), P("rows", None, None), P())
    return jax.shard_map(
        shards, mesh=mesh, in_specs=placed, out_specs=P("rows", "jpair"), check_vma=False
    )
```

```python
import functools

import jax
import jax.numpy as jnp
from jax import lax
from jax.experimental import pallas as pl
from jax.experimental.pallas import tpu as pltpu
from jax.sharding import PartitionSpec as P

BLK = 256
LANES = 128
MESH = pl.DeviceIdType.MESH
RING = 4
GROUP = 4
LATE = 16
Y_TYPE = jnp.bfloat16
Z_TYPE = jnp.bfloat16


def kernel(
    cols_all, low, high, dip, out,
    g_a, g_b, d_buf, low_buf, low_t, applied, tile_a, tile_b, sib_buf, y_send, y_recv, z_send, z_recv,
    recv_g, send_g, recv_low, send_low, recv_sum, send_sum, local_sem, cols,
    g_late, early, late_parts, late_list, across_here,
):
    gathered = (g_a, g_b)
    tiles = (tile_a, tile_b)
    jp = lax.axis_index("jpair")
    rw = lax.axis_index("rows")
    x, zh = lax.rem(jp, RING), lax.div(jp, RING)
    c, y, z = lax.rem(rw, 2), lax.rem(lax.div(rw, 2), RING), lax.div(rw, 2 * RING)

    def rows_of(zs, ys, cs):
        return (zs * RING + ys) * 2 + cs

    def ring(v, step):
        return lax.rem(v + step + RING, RING)

    def at_rows(zs, ys, cs):
        return (jp, rows_of(zs, ys, cs))

    def at_jpair(zhs, xs):
        return (zhs * RING + xs, rw)

    right, left = at_rows(z, ring(y, 1), c), at_rows(z, ring(y, -1), c)
    sibling = at_rows(z, y, 1 - c)
    y_others = [at_rows(z, ring(y, d), c) for d in (1, 2, 3)]
    z_others = [at_rows(ring(z, d), y, c) for d in (1, 2, 3)]
    x_others = [at_jpair(zh, ring(x, d)) for d in (1, 2, 3)]
    across = at_jpair(1 - zh, x)

    barrier = pltpu.get_barrier_semaphore()
    partners = [y_others[0], y_others[2], z_others[0], z_others[2], sibling, y_others[1], z_others[1]] + x_others
    for partner in partners:
        pl.semaphore_signal(barrier, inc=1, device_id=partner, device_id_type=MESH)

    @pl.when(zh == 0)
    def _():
        pl.semaphore_signal(barrier, inc=1, device_id=across, device_id_type=MESH)
        pl.semaphore_wait(barrier, len(partners))

    @pl.when(zh == 1)
    def _():
        pl.semaphore_wait(barrier, len(partners) + 1)
        pl.semaphore_signal(across_here, inc=1, device_id=across, device_id_type=MESH)

    waits = {}

    def remote(src, dst, send_sem, recv_sem, target):
        return pltpu.make_async_remote_copy(
            src_ref=src, dst_ref=dst, send_sem=send_sem, recv_sem=recv_sem,
            device_id=target, device_id_type=MESH,
        )

    inner = jnp.logical_and(z > 0, z < RING - 1)
    slots = {}

    def piece(h, r, half, n=1):
        return gathered[h].at[pl.ds(r * 4 + 2 * half, 2 * n)]

    def is_late(h, g):
        return h == 1 and g >= 2

    def late_piece(g, core, half, n=1):
        return g_late.at[pl.ds(((g - 2) * 2 + core) * 4 + 2 * half, 2 * n)]

    def send(key, h, r, half, target, src=None, n=1, cond=None, dst=None):
        dst = piece(h, r, half, n) if dst is None else dst
        sem = send_g.at[h, slots.setdefault((h, key), sum(k[0] == h for k in slots))]
        copy = remote(dst if src is None else src, dst, sem, recv_g.at[h, r, half], target)
        copy.start()
        waits[(h, key)] = (int(2 * n), cond)

    def arrive(h, r, half, n=1, ref=None):
        ref = piece(h, r, half, n) if ref is None else ref
        remote(ref, ref, send_g.at[h, 0], recv_g.at[h, r, half], sibling).wait_recv()

    def own_part(h, half, n=1):
        return high.at[pl.ds(2 * half, 2 * n), :, pl.ds(LANES * h, LANES)]

    onward = at_rows(jnp.where(z == RING - 1, z - 1, z + 1), y, c)
    downward = at_rows(ring(z, -1), y, c)
    sources = [z, z + 1 - 2 * lax.rem(z, 2), jnp.where(z < 2, 2, 1), jnp.where(z < 2, 3, 0)]

    def own_z(h, is_inner):
        for half in (0, 1):
            send(("own_z", half, 0), h, rw, half, onward, own_part(h, half))
            if is_inner:
                send(("own_z", half, 1), h, rw, half, downward, own_part(h, half), cond=inner)

    def own_y(h, is_inner):
        for half in (0, 1):
            send(("own_y", half, 0), h, rw, half, right, own_part(h, half))
            send(("own_y", 1 - half, 1), h, rw, 1 - half, left, own_part(h, 1 - half))
        send(("own_s",), h, rw, 0, sibling, own_part(h, 0, 2), n=2)

    def from_z(h, g, is_inner, halves=(0, 1)):
        zs = sources[g]
        r = rows_of(zs, y, c)
        target = at_rows(jnp.where(zs < z, lax.rem(z + 1, RING), ring(z, -1)), y, c)
        for half in halves:
            arrive(h, r, half)
            if is_inner:
                send(("z_z", g, half), h, r, half, target, cond=inner)
            send(("z_y", g, half, 0), h, r, half, right)
            send(("z_y", g, half, 1), h, r, half, left)
        if 1 in halves:
            send(("z_s", g), h, r, 0, sibling, n=2)

    def from_two(h, g, is_inner):
        for half in (0, 1):
            from_z(h, g, is_inner, (half,))
            from_z(h, g + 1, is_inner, (half,))

    def from_y(h, g, is_inner):
        r_left = rows_of(sources[g], ring(y, -1), c)
        r_right = rows_of(sources[g], ring(y, 1), c)
        arrive(h, r_left, 0)
        forward(("y_y", g, 0), h, g, r_left, 0, right)
        arrive(h, r_right, 1)
        forward(("y_y", g, 1), h, g, r_right, 1, left)
        arrive(h, r_left, 1)
        send(("y_s", g, 0), h, r_left, 0, sibling, n=2)
        arrive(h, r_right, 0)
        send(("y_s", g, 1), h, r_right, 0, sibling, n=2)

    def by_z(h, g):
        return g == 1 and h == 1

    partner = at_rows(z + 1 - 2 * lax.rem(z, 2), y, c)

    def part_of(h, r, k, n):
        return gathered[h].at[pl.ds(r * 4 + k, n)]

    def forward(key, h, g, r, half, target):
        src = piece(h, r, half) if not by_z(h, g) else part_of(h, r, 3 * half, 1)
        dst = late_piece(g, c, half) if is_late(h, g) else src
        send(key, h, r, half, target, src=src, dst=dst, n=0.5 if by_z(h, g) else 1)

    def from_far(h, g, is_inner):
        r = rows_of(sources[g], ring(y, 2), c)
        for half in (0, 1):
            ref = late_piece(g, c, half) if is_late(h, g) else None
            arrive(h, r, half, ref=part_of(h, r, 3 * half, 1) if by_z(h, g) else ref)
        middle = part_of(h, r, 1, 2)
        if g == 0 and by_z(h, 1):
            send(("f_z",), h, r, 2, partner, src=middle, dst=middle)
        if by_z(h, g):
            arrive(h, r, 2, ref=middle)
        whole = late_piece(g, c, 0, 2) if is_late(h, g) else None
        send(("f_s", g), h, r, 0, sibling, n=2, src=whole, dst=whole)

    def from_sibling(h, late):
        for g in range(RING):
            for d in range(RING):
                if late != (is_late(h, g) and d == 2):
                    continue
                ref = late_piece(g, 1 - c, 0, 2) if late else None
                arrive(h, rows_of(sources[g], ring(y, d), 1 - c), 0, 2, ref)

    def local_part(h):
        copy = pltpu.make_async_copy(
            high.at[:, :, pl.ds(LANES * h, LANES)], gathered[h].at[pl.ds(rw * 4, 4)], local_sem.at[h]
        )
        copy.start()
        return copy

    def by_place(inner_steps, end_steps):
        for is_inner, steps in ((True, inner_steps), (False, end_steps)):

            @pl.when(inner if is_inner else jnp.logical_not(inner))
            def _(is_inner=is_inner, steps=steps):
                for step in steps:
                    step[0](*step[1:], is_inner)

    LOW_PARTS = 4

    def send_low_to(key, j, target, src, part):
        dst = low_buf.at[j, pl.ds(part * 256, 256)]
        if src is None:
            src = dst
        sem = send_low.at[slots.setdefault(("low", key), sum(k[0] == "low" for k in slots))]
        copy = remote(src, dst, sem, recv_low.at[j, part], target)
        copy.start()
        waits[("low", key)] = (0, None)

    def arrive_low(j, part):
        dst = low_buf.at[j, pl.ds(part * 256, 256)]
        remote(dst, dst, send_low.at[0], recv_low.at[j, part], sibling).wait_recv()

    j_across = (1 - zh) * RING + x

    def low_x(is_inner):
        for part in range(LOW_PARTS):
            for d in range(3):
                send_low_to(("x", d, part), jp, x_others[d], low.at[pl.ds(part * 256, 256)], part)

    def low_across(part, is_inner):
        if part == 0:

            @pl.when(zh == 0)
            def _():
                pl.semaphore_wait(across_here, 1)

        send_low_to(("across", part), jp, across, low.at[pl.ds(part * 256, 256)], part)

    def low_onward(part, is_inner):
        arrive_low(j_across, part)
        for d in range(3):
            send_low_to(("onward", d, part), j_across, x_others[d], None, part)

    def low_arrive(zhs):
        for part in range(LOW_PARTS):
            for d in (1, 2, 3):
                arrive_low(zhs * RING + ring(x, d), part)

    def low_turn(zhs):
        def one(i, _):
            j = zhs * RING + i
            low_t[pl.ds(pl.multiple_of(j * BLK, BLK), BLK), :] = low_buf[j].T
            return 0

        lax.fori_loop(0, RING, one, 0)

    def place_of(b):
        col = cols[rw * 64 + b]
        chip = lax.shift_right_logical(col, 3)
        late_2 = chip == sources[2] * RING + ring(y, 2)
        late_3 = chip == sources[3] * RING + ring(y, 2)
        return col, jnp.logical_or(late_2, late_3), jnp.bitwise_and(col, 7) + 8 * late_3.astype(jnp.int32)

    def block_of(h, b):
        col, late, _ = place_of(b)
        return gathered[h][col if h == 0 else jnp.where(late, 128, col)]

    def apply_rows(h, q0, n):
        def row(q, _):
            def some(i, total):
                b = q * 16 + i * GROUP
                lhs = jnp.concatenate([d_buf[b + k] for k in range(GROUP)], axis=1)
                rhs = jnp.concatenate([block_of(h, b + k) for k in range(GROUP)], axis=0)
                return total + jnp.dot(lhs, rhs, preferred_element_type=jnp.float32)

            total = lax.fori_loop(0, 16 // GROUP, some, jnp.zeros((BLK, LANES), jnp.float32))
            here = pl.ds(pl.multiple_of(q * BLK, BLK), BLK)
            if h == 0:
                applied[h, here, :] = total.astype(jnp.bfloat16)
            else:
                early[here, :] = total
            return 0

        lax.fori_loop(q0, q0 + n, row, 0)

    def list_late():
        def one(b, carry):
            count, found = carry[0], carry[1:]
            _, late, _ = place_of(b)
            found = tuple(jnp.where(jnp.logical_and(late, count == i), b, f) for i, f in enumerate(found))
            return (count + late.astype(jnp.int32),) + found

        carry = (jnp.int32(0),) + (jnp.int32(0),) * LATE
        for q in range(4):
            late_list[LATE + q] = jnp.minimum(carry[0], LATE)
            carry = lax.fori_loop(16 * q, 16 * q + 16, one, carry)
        late_list[LATE + 4] = jnp.minimum(carry[0], LATE)
        for i in range(LATE):
            late_list[i] = carry[1 + i]

    def apply_late():
        late_parts[0] = jnp.zeros((BLK, LANES), jnp.float32)

        def one(i, total):
            for k in range(4):
                b = jnp.bitwise_and(late_list[4 * i + k], 63)
                _, _, at = place_of(b)
                total = total + jnp.dot(d_buf[b], g_late[at], preferred_element_type=jnp.float32)
                late_parts[4 * i + k + 1] = total
            return total

        lax.fori_loop(0, LATE // 4, one, jnp.zeros((BLK, LANES), jnp.float32))
        for q in range(4):
            here = pl.ds(q * BLK, BLK)
            first, last = (jnp.clip(late_list[LATE + q + k], 0, LATE) for k in (0, 1))
            total = early[here, :] + (late_parts[last] - late_parts[first])
            applied[1, here, :] = total.astype(jnp.bfloat16)

    quarters = [3 - z, jnp.where(z < 2, z + 2, z - 2), z + 1 - 2 * lax.rem(z, 2), z]

    def sum_copy(h, k, src, dst, target):
        return remote(src, dst, send_sum.at[h, k], recv_sum.at[h, k], target)

    def sib_copy(h, i):
        part = pl.ds(4 * quarters[i], 4)
        return sum_copy(h, i, tiles[h].at[part, 1 - c], sib_buf.at[h, part], sibling)

    def y_copy(h, i, d):
        return sum_copy(h, 3 + 3 * i + d, y_send.at[h, d, i], y_recv.at[h, d, i], y_others[d - 1])

    def z_copy(h, i):
        return sum_copy(h, 16 + i, z_send.at[h, i], z_recv.at[h, i], at_rows(quarters[i], y, c))

    def tile_quarters(h, i0, n):
        def one(i, _):
            quarter = jnp.where(i < 2, jnp.where(i == 0, quarters[0], quarters[1]), jnp.where(i == 2, quarters[2], z))
            rows = pl.ds(pl.multiple_of(quarter * 512, 512), 512)
            part = jnp.dot(low_t[rows, :], applied[h], preferred_element_type=jnp.float32)
            tiles[h][pl.ds(4 * quarter, 4)] = part.reshape(4, 2, 64, LANES)
            if h == 1:
                at = pl.ds(4 * quarter, 4)
                sum_copy(h, i, tiles[h].at[at, 1 - c], sib_buf.at[h, at], sibling).start()
            return 0

        lax.fori_loop(i0, i0 + n, one, 0)

    def y_quarter(h, i):
        sib_copy(h, i).wait()
        for d in (2, 1, 3):
            p = quarters[i] * 4 + ring(y, d)
            y_send[h, d, i] = (tiles[h][p, c] + sib_buf[h, p]).astype(Y_TYPE)
            y_copy(h, i, d).start()

    def z_quarter(h, i):
        if h == 1:
            for d in (1, 2, 3):
                y_copy(h, i, d).wait()
        p = quarters[i] * 4 + y
        total = tiles[h][p, c] + sib_buf[h, p]
        for d in (1, 2, 3):
            total = total + y_recv[h, d, i].astype(jnp.float32)
        if i == 3:
            return total
        z_send[h, i] = total.astype(Z_TYPE)
        z_copy(h, i).start()

    def sib_whole():
        return sum_copy(0, 0, tiles[0].at[:, 1 - c], sib_buf.at[0], sibling)

    def y_whole(d):
        return sum_copy(0, 3 + d, y_send.at[0, d], y_recv.at[0, d], y_others[d - 1])

    def tile_whole():
        tile_quarters(0, 0, 4)
        sib_whole().start()

    def y_whole_fill():
        sib_whole().wait()
        for d in (2, 1, 3):
            for i in range(4):
                p = quarters[i] * 4 + ring(y, d)
                y_send[0, d, i] = (tiles[0][p, c] + sib_buf[0, p]).astype(Y_TYPE)

    def y_whole_start():
        for d in (2, 1, 3):
            y_whole(d).start()

    def y_whole_wait():
        for d in (2, 1, 3):
            y_whole(d).wait()

    def sum_end(h, total):
        for i in range(3):
            z_copy(h, i).wait()
            total = total + z_recv[h, i].astype(jnp.float32)
        out[:, LANES * h : LANES * (h + 1)] = total

    cols_copy = pltpu.make_async_copy(cols_all, cols, local_sem.at[4])
    cols_copy.start()
    by_place([(own_z, 0), (own_y, 0)], [(own_z, 0), (own_y, 0)])
    local_0 = local_part(0)
    low_x(None)
    own_low = pltpu.make_async_copy(low, low_buf.at[jp], local_sem.at[2])
    own_low.start()
    dip_copy = pltpu.make_async_copy(dip, d_buf, local_sem.at[3])
    dip_copy.start()
    local_1 = local_part(1)
    gathered[1][128] = jnp.zeros((BLK, LANES), jnp.bfloat16)
    cols_copy.wait()
    list_late()
    by_place(
        [(from_two, 0, 1), (low_across, 0), (from_y, 0, 0), (from_z, 0, 3), (low_across, 1), (low_across, 2), (from_y, 0, 1), (from_far, 0, 0),
         (from_y, 0, 2), (own_y, 1), (own_z, 1), (low_across, 3), (low_onward, 0), (from_far, 0, 1)],
        [(from_z, 0, 1), (from_y, 0, 0), (from_y, 0, 1), (from_z, 0, 2), (low_across, 0), (from_far, 0, 0), (from_z, 0, 3), (low_across, 1), (low_across, 2),
         (from_y, 0, 2), (from_far, 0, 1), (own_y, 1), (own_z, 1), (low_across, 3), (low_onward, 0)],
    )
    own_low.wait()
    low_arrive(zh)
    low_turn(zh)
    by_place(
        [(from_y, 0, 3), (low_onward, 1), (from_far, 0, 2), (from_two, 1, 1), (from_far, 0, 3)],
        [(from_y, 0, 3), (low_onward, 1), (from_far, 0, 2), (from_z, 1, 1), (from_far, 0, 3)],
    )
    from_sibling(0, False)
    local_0.wait()
    dip_copy.wait()
    by_place([(from_y, 1, 0), (low_onward, 2), (from_z, 1, 3)], [(from_y, 1, 0), (low_onward, 2), (from_z, 1, 2)])
    apply_rows(0, 0, 2)
    by_place([(from_y, 1, 1)], [(from_y, 1, 1)])
    apply_rows(0, 2, 2)
    by_place([(from_far, 1, 0)], [(from_z, 1, 3), (from_far, 1, 0)])
    low_onward(3, None)
    by_place([(from_y, 1, 2)], [(from_y, 1, 2)])
    by_place([(from_far, 1, 1)], [(from_far, 1, 1)])
    low_arrive(1 - zh)
    low_turn(1 - zh)
    by_place([(from_y, 1, 3)], [(from_y, 1, 3)])
    tile_whole()
    y_whole_fill()
    y_whole_start()
    from_sibling(1, False)
    local_1.wait()
    apply_rows(1, 0, 2)
    by_place([(from_far, 1, 2)], [(from_far, 1, 2)])
    apply_rows(1, 2, 2)
    by_place([(from_far, 1, 3)], [(from_far, 1, 3)])
    from_sibling(1, True)
    apply_late()
    tile_quarters(1, 0, 3)
    y_quarter(1, 0)
    y_quarter(1, 1)
    y_quarter(1, 2)
    tile_quarters(1, 3, 1)
    y_quarter(1, 3)
    y_whole_wait()
    mine_0 = [z_quarter(0, i) for i in range(4)][3]
    z_quarter(1, 0)
    z_quarter(1, 1)
    z_quarter(1, 2)
    mine_1 = z_quarter(1, 3)
    sum_end(0, mine_0)
    for (h, key), (n, cond) in waits.items():
        slot = slots[(h, key)]
        if h == "low":
            ref = low_buf.at[0, pl.ds(0, 256)]
            copy = remote(ref, ref, send_low.at[slot], recv_low.at[0, 0], sibling)
        else:
            ref = gathered[h].at[pl.ds(0, n)]
            copy = remote(ref, ref, send_g.at[h, slot], recv_g.at[h, 0, 0], sibling)
        if cond is None:
            copy.wait_send()
        else:
            pl.when(cond)(copy.wait_send)
    sum_end(1, mine_1)


def shards(psi_low, psi_high, dip_blocks, block_cols):
    any_space = pl.BlockSpec(memory_space=pl.ANY)
    return pl.pallas_call(
        kernel,
        out_shape=pltpu.VMEM((64, 256), jnp.float32),
        in_specs=[any_space] * 4,
        out_specs=pl.BlockSpec(memory_space=pltpu.VMEM),
        scratch_shapes=[
            pltpu.VMEM((128, BLK, LANES), jnp.bfloat16),
            pltpu.VMEM((129, BLK, LANES), jnp.bfloat16),
            pltpu.VMEM((64, BLK, BLK), jnp.bfloat16),
            pltpu.VMEM((8, 1024, 256), jnp.bfloat16),
            pltpu.VMEM((2048, 1024), jnp.bfloat16),
            pltpu.VMEM((2, 1024, LANES), jnp.bfloat16),
            pltpu.VMEM((16, 2, 64, LANES), jnp.float32),
            pltpu.VMEM((16, 2, 64, LANES), jnp.float32),
            pltpu.VMEM((2, 16, 64, LANES), jnp.float32),
            pltpu.VMEM((2, 4, 4, 64, LANES), Y_TYPE),
            pltpu.VMEM((2, 4, 4, 64, LANES), Y_TYPE),
            pltpu.VMEM((2, 4, 64, LANES), Z_TYPE),
            pltpu.VMEM((2, 4, 64, LANES), Z_TYPE),
            pltpu.SemaphoreType.DMA((2, 32, 3)),
            pltpu.SemaphoreType.DMA((2, 72)),
            pltpu.SemaphoreType.DMA((8, 4)),
            pltpu.SemaphoreType.DMA((32,)),
            pltpu.SemaphoreType.DMA((2, 20)),
            pltpu.SemaphoreType.DMA((2, 20)),
            pltpu.SemaphoreType.DMA((5,)),
            pltpu.SMEM((2048,), jnp.int32),
            pltpu.VMEM((LATE, BLK, LANES), jnp.bfloat16),
            pltpu.VMEM((1024, LANES), jnp.float32),
            pltpu.VMEM((LATE + 1, BLK, LANES), jnp.float32),
            pltpu.SMEM((LATE + 5,), jnp.int32),
            pltpu.SemaphoreType.REGULAR,
        ],
        compiler_params=pltpu.CompilerParams(
            collective_id=0, has_side_effects=True, vmem_limit_bytes=56 * 1024 * 1024
        ),
        cost_estimate=pl.CostEstimate(flops=3 * 2**30, bytes_accessed=10 * 2**20, transcendentals=0),
    )(block_cols, psi_low, psi_high.reshape(4, BLK, 256), dip_blocks)


def solution(mesh):
    placed = (P("rows", "jpair"), P("rows", "jpair"), P("rows", None, None), P())
    return jax.shard_map(
        shards, mesh=mesh, in_specs=placed, out_specs=P("rows", "jpair"), check_vma=False
    )
```

```python
import functools

import jax
import jax.numpy as jnp
from jax import lax
from jax.experimental import pallas as pl
from jax.experimental.pallas import tpu as pltpu
from jax.sharding import PartitionSpec as P

BLK = 256
LANES = 128
MESH = pl.DeviceIdType.MESH
RING = 4
GROUP = 4
LATE = 16
Y_TYPE = jnp.bfloat16
Z_TYPE = jnp.bfloat16


def kernel(
    cols_all, low, high, dip, out,
    g_a, g_b, d_buf, low_buf, low_t, applied, tile_a, tile_b, sib_buf, y_send, y_recv, z_send, z_recv,
    recv_g, send_g, recv_low, send_low, recv_sum, send_sum, local_sem, cols,
    g_late, early, late_parts, late_list, across_here,
):
    gathered = (g_a, g_b)
    tiles = (tile_a, tile_b)
    jp = lax.axis_index("jpair")
    rw = lax.axis_index("rows")
    x, zh = lax.rem(jp, RING), lax.div(jp, RING)
    c, y, z = lax.rem(rw, 2), lax.rem(lax.div(rw, 2), RING), lax.div(rw, 2 * RING)

    def rows_of(zs, ys, cs):
        return (zs * RING + ys) * 2 + cs

    def ring(v, step):
        return lax.rem(v + step + RING, RING)

    def at_rows(zs, ys, cs):
        return (jp, rows_of(zs, ys, cs))

    def at_jpair(zhs, xs):
        return (zhs * RING + xs, rw)

    right, left = at_rows(z, ring(y, 1), c), at_rows(z, ring(y, -1), c)
    sibling = at_rows(z, y, 1 - c)
    y_others = [at_rows(z, ring(y, d), c) for d in (1, 2, 3)]
    z_others = [at_rows(ring(z, d), y, c) for d in (1, 2, 3)]
    x_others = [at_jpair(zh, ring(x, d)) for d in (1, 2, 3)]
    across = at_jpair(1 - zh, x)

    barrier = pltpu.get_barrier_semaphore()
    partners = [y_others[0], y_others[2], z_others[0], z_others[2], sibling, y_others[1], z_others[1]] + x_others
    for partner in partners:
        pl.semaphore_signal(barrier, inc=1, device_id=partner, device_id_type=MESH)

    @pl.when(zh == 0)
    def _():
        pl.semaphore_signal(barrier, inc=1, device_id=across, device_id_type=MESH)
        pl.semaphore_wait(barrier, len(partners))

    @pl.when(zh == 1)
    def _():
        pl.semaphore_wait(barrier, len(partners) + 1)
        pl.semaphore_signal(across_here, inc=1, device_id=across, device_id_type=MESH)

    waits = {}

    def remote(src, dst, send_sem, recv_sem, target):
        return pltpu.make_async_remote_copy(
            src_ref=src, dst_ref=dst, send_sem=send_sem, recv_sem=recv_sem,
            device_id=target, device_id_type=MESH,
        )

    inner = jnp.logical_and(z > 0, z < RING - 1)
    slots = {}

    def piece(h, r, half, n=1):
        return gathered[h].at[pl.ds(r * 4 + 2 * half, 2 * n)]

    def is_late(h, g):
        return h == 1 and g >= 2

    def late_piece(g, core, half, n=1):
        return g_late.at[pl.ds(((g - 2) * 2 + core) * 4 + 2 * half, 2 * n)]

    def send(key, h, r, half, target, src=None, n=1, cond=None, dst=None):
        dst = piece(h, r, half, n) if dst is None else dst
        sem = send_g.at[h, slots.setdefault((h, key), sum(k[0] == h for k in slots))]
        copy = remote(dst if src is None else src, dst, sem, recv_g.at[h, r, half], target)
        copy.start()
        waits[(h, key)] = (int(2 * n), cond)

    def arrive(h, r, half, n=1, ref=None):
        ref = piece(h, r, half, n) if ref is None else ref
        remote(ref, ref, send_g.at[h, 0], recv_g.at[h, r, half], sibling).wait_recv()

    def own_part(h, half, n=1):
        return high.at[pl.ds(2 * half, 2 * n), :, pl.ds(LANES * h, LANES)]

    onward = at_rows(jnp.where(z == RING - 1, z - 1, z + 1), y, c)
    downward = at_rows(ring(z, -1), y, c)
    sources = [z, z + 1 - 2 * lax.rem(z, 2), jnp.where(z < 2, 2, 1), jnp.where(z < 2, 3, 0)]

    def own_z(h, is_inner):
        for half in (0, 1):
            send(("own_z", half, 0), h, rw, half, onward, own_part(h, half))
            if is_inner:
                send(("own_z", half, 1), h, rw, half, downward, own_part(h, half), cond=inner)

    def own_y(h, is_inner):
        for half in (0, 1):
            send(("own_y", half, 0), h, rw, half, right, own_part(h, half))
            send(("own_y", 1 - half, 1), h, rw, 1 - half, left, own_part(h, 1 - half))
        send(("own_s",), h, rw, 0, sibling, own_part(h, 0, 2), n=2)

    def from_z(h, g, is_inner, halves=(0, 1)):
        zs = sources[g]
        r = rows_of(zs, y, c)
        target = at_rows(jnp.where(zs < z, lax.rem(z + 1, RING), ring(z, -1)), y, c)
        for half in halves:
            arrive(h, r, half)
            if is_inner:
                send(("z_z", g, half), h, r, half, target, cond=inner)
            send(("z_y", g, half, 0), h, r, half, right)
            send(("z_y", g, half, 1), h, r, half, left)
        if 1 in halves:
            send(("z_s", g), h, r, 0, sibling, n=2)

    def from_two(h, g, is_inner):
        for half in (0, 1):
            from_z(h, g, is_inner, (half,))
            from_z(h, g + 1, is_inner, (half,))

    def from_y(h, g, is_inner):
        r_left = rows_of(sources[g], ring(y, -1), c)
        r_right = rows_of(sources[g], ring(y, 1), c)
        arrive(h, r_left, 0)
        forward(("y_y", g, 0), h, g, r_left, 0, right)
        arrive(h, r_right, 1)
        forward(("y_y", g, 1), h, g, r_right, 1, left)
        arrive(h, r_left, 1)
        send(("y_s", g, 0), h, r_left, 0, sibling, n=2)
        arrive(h, r_right, 0)
        send(("y_s", g, 1), h, r_right, 0, sibling, n=2)

    def by_z(h, g):
        return g == 1 and h == 1

    partner = at_rows(z + 1 - 2 * lax.rem(z, 2), y, c)

    def part_of(h, r, k, n):
        return gathered[h].at[pl.ds(r * 4 + k, n)]

    def forward(key, h, g, r, half, target):
        src = piece(h, r, half) if not by_z(h, g) else part_of(h, r, 3 * half, 1)
        dst = late_piece(g, c, half) if is_late(h, g) else src
        send(key, h, r, half, target, src=src, dst=dst, n=0.5 if by_z(h, g) else 1)

    def from_far(h, g, is_inner):
        r = rows_of(sources[g], ring(y, 2), c)
        for half in (0, 1):
            ref = late_piece(g, c, half) if is_late(h, g) else None
            arrive(h, r, half, ref=part_of(h, r, 3 * half, 1) if by_z(h, g) else ref)
        middle = part_of(h, r, 1, 2)
        if g == 0 and by_z(h, 1):
            send(("f_z",), h, r, 2, partner, src=middle, dst=middle)
        if by_z(h, g):
            arrive(h, r, 2, ref=middle)
        whole = late_piece(g, c, 0, 2) if is_late(h, g) else None
        send(("f_s", g), h, r, 0, sibling, n=2, src=whole, dst=whole)

    def from_sibling(h, late):
        for g in range(RING):
            for d in range(RING):
                if late != (is_late(h, g) and d == 2):
                    continue
                ref = late_piece(g, 1 - c, 0, 2) if late else None
                arrive(h, rows_of(sources[g], ring(y, d), 1 - c), 0, 2, ref)

    def local_part(h):
        copy = pltpu.make_async_copy(
            high.at[:, :, pl.ds(LANES * h, LANES)], gathered[h].at[pl.ds(rw * 4, 4)], local_sem.at[h]
        )
        copy.start()
        return copy

    def by_place(inner_steps, end_steps):
        for is_inner, steps in ((True, inner_steps), (False, end_steps)):

            @pl.when(inner if is_inner else jnp.logical_not(inner))
            def _(is_inner=is_inner, steps=steps):
                for step in steps:
                    step[0](*step[1:], is_inner)

    LOW_PARTS = 4

    def send_low_to(key, j, target, src, part):
        dst = low_buf.at[j, pl.ds(part * 256, 256)]
        if src is None:
            src = dst
        sem = send_low.at[slots.setdefault(("low", key), sum(k[0] == "low" for k in slots))]
        copy = remote(src, dst, sem, recv_low.at[j, part], target)
        copy.start()
        waits[("low", key)] = (0, None)

    def arrive_low(j, part):
        dst = low_buf.at[j, pl.ds(part * 256, 256)]
        remote(dst, dst, send_low.at[0], recv_low.at[j, part], sibling).wait_recv()

    j_across = (1 - zh) * RING + x

    def low_x(is_inner):
        for part in range(LOW_PARTS):
            for d in range(3):
                send_low_to(("x", d, part), jp, x_others[d], low.at[pl.ds(part * 256, 256)], part)

    def low_across(part, is_inner):
        if part == 0:

            @pl.when(zh == 0)
            def _():
                pl.semaphore_wait(across_here, 1)

        send_low_to(("across", part), jp, across, low.at[pl.ds(part * 256, 256)], part)

    def low_onward(part, is_inner):
        arrive_low(j_across, part)
        for d in range(3):
            send_low_to(("onward", d, part), j_across, x_others[d], None, part)

    def low_arrive(zhs):
        for part in range(LOW_PARTS):
            for d in (1, 2, 3):
                arrive_low(zhs * RING + ring(x, d), part)

    def low_turn(zhs):
        def one(i, _):
            j = zhs * RING + i
            low_t[pl.ds(pl.multiple_of(j * BLK, BLK), BLK), :] = low_buf[j].T
            return 0

        lax.fori_loop(0, RING, one, 0)

    def place_of(b):
        col = cols[rw * 64 + b]
        chip = lax.shift_right_logical(col, 3)
        late_2 = chip == sources[2] * RING + ring(y, 2)
        late_3 = chip == sources[3] * RING + ring(y, 2)
        return col, jnp.logical_or(late_2, late_3), jnp.bitwise_and(col, 7) + 8 * late_3.astype(jnp.int32)

    def block_of(h, b):
        col, late, _ = place_of(b)
        return gathered[h][col if h == 0 else jnp.where(late, 128, col)]

    def apply_rows(h, q0, n):
        def row(q, _):
            def some(i, total):
                b = q * 16 + i * GROUP
                lhs = jnp.concatenate([d_buf[b + k] for k in range(GROUP)], axis=1)
                rhs = jnp.concatenate([block_of(h, b + k) for k in range(GROUP)], axis=0)
                return total + jnp.dot(lhs, rhs, preferred_element_type=jnp.float32)

            total = lax.fori_loop(0, 16 // GROUP, some, jnp.zeros((BLK, LANES), jnp.float32))
            here = pl.ds(pl.multiple_of(q * BLK, BLK), BLK)
            if h == 0:
                applied[h, here, :] = total.astype(jnp.bfloat16)
            else:
                early[here, :] = total
            return 0

        lax.fori_loop(q0, q0 + n, row, 0)

    def list_late():
        def one(b, carry):
            count, found = carry[0], carry[1:]
            _, late, _ = place_of(b)
            found = tuple(jnp.where(jnp.logical_and(late, count == i), b, f) for i, f in enumerate(found))
            return (count + late.astype(jnp.int32),) + found

        carry = (jnp.int32(0),) + (jnp.int32(0),) * LATE
        for q in range(4):
            late_list[LATE + q] = jnp.minimum(carry[0], LATE)
            carry = lax.fori_loop(16 * q, 16 * q + 16, one, carry)
        late_list[LATE + 4] = jnp.minimum(carry[0], LATE)
        for i in range(LATE):
            late_list[i] = carry[1 + i]

    def apply_late():
        late_parts[0] = jnp.zeros((BLK, LANES), jnp.float32)

        def one(i, total):
            for k in range(4):
                b = jnp.bitwise_and(late_list[4 * i + k], 63)
                _, _, at = place_of(b)
                total = total + jnp.dot(d_buf[b], g_late[at], preferred_element_type=jnp.float32)
                late_parts[4 * i + k + 1] = total
            return total

        lax.fori_loop(0, LATE // 4, one, jnp.zeros((BLK, LANES), jnp.float32))
        for q in range(4):
            here = pl.ds(q * BLK, BLK)
            first, last = (jnp.clip(late_list[LATE + q + k], 0, LATE) for k in (0, 1))
            total = early[here, :] + (late_parts[last] - late_parts[first])
            applied[1, here, :] = total.astype(jnp.bfloat16)

    quarters = [3 - z, jnp.where(z < 2, z + 2, z - 2), z + 1 - 2 * lax.rem(z, 2), z]

    def sum_copy(h, k, src, dst, target):
        return remote(src, dst, send_sum.at[h, k], recv_sum.at[h, k], target)

    def sib_copy(h, i):
        part = pl.ds(4 * quarters[i], 4)
        return sum_copy(h, i, tiles[h].at[part, 1 - c], sib_buf.at[h, part], sibling)

    def y_copy(h, i, d):
        return sum_copy(h, 3 + 3 * i + d, y_send.at[h, d, i], y_recv.at[h, d, i], y_others[d - 1])

    def z_copy(h, i):
        return sum_copy(h, 16 + i, z_send.at[h, i], z_recv.at[h, i], at_rows(quarters[i], y, c))

    def tile_quarters(h, i0, n, first=None):
        def one(i, _):
            quarter = first + i if h == 0 else jnp.where(i < 2, jnp.where(i == 0, quarters[0], quarters[1]), jnp.where(i == 2, quarters[2], z))
            rows = pl.ds(pl.multiple_of(quarter * 512, 512), 512)
            part = jnp.dot(low_t[rows, :], applied[h], preferred_element_type=jnp.float32)
            tiles[h][pl.ds(4 * quarter, 4)] = part.reshape(4, 2, 64, LANES)
            if h == 1:
                at = pl.ds(4 * quarter, 4)
                sum_copy(h, i, tiles[h].at[at, 1 - c], sib_buf.at[h, at], sibling).start()
            return 0

        lax.fori_loop(i0, i0 + n, one, 0)

    def y_quarter(h, i):
        sib_copy(h, i).wait()
        for d in (2, 1, 3):
            p = quarters[i] * 4 + ring(y, d)
            y_send[h, d, i] = (tiles[h][p, c] + sib_buf[h, p]).astype(Y_TYPE)
            y_copy(h, i, d).start()

    def z_quarter(h, i):
        if h == 1:
            for d in (1, 2, 3):
                y_copy(h, i, d).wait()
        p = quarters[i] * 4 + y
        total = tiles[h][p, c] + sib_buf[h, p]
        for d in (1, 2, 3):
            total = total + y_recv[h, d, i].astype(jnp.float32)
        if i == 3:
            return total
        z_send[h, i] = total.astype(Z_TYPE)
        z_copy(h, i).start()

    def sib_whole():
        return sum_copy(0, 0, tiles[0].at[:, 1 - c], sib_buf.at[0], sibling)

    def y_whole(d):
        return sum_copy(0, 3 + d, y_send.at[0, d], y_recv.at[0, d], y_others[d - 1])

    def tile_half(zhs):
        tile_quarters(0, 0, 2, 2 * zhs)

    def y_whole_fill():
        sib_whole().wait()
        for d in (2, 1, 3):
            for i in range(4):
                p = quarters[i] * 4 + ring(y, d)
                y_send[0, d, i] = (tiles[0][p, c] + sib_buf[0, p]).astype(Y_TYPE)

    def y_whole_start():
        for d in (2, 1, 3):
            y_whole(d).start()

    def y_whole_wait():
        for d in (2, 1, 3):
            y_whole(d).wait()

    def sum_end(h, total):
        for i in range(3):
            z_copy(h, i).wait()
            total = total + z_recv[h, i].astype(jnp.float32)
        out[:, LANES * h : LANES * (h + 1)] = total

    cols_copy = pltpu.make_async_copy(cols_all, cols, local_sem.at[4])
    cols_copy.start()
    by_place([(own_z, 0), (own_y, 0)], [(own_z, 0), (own_y, 0)])
    local_0 = local_part(0)
    low_x(None)
    own_low = pltpu.make_async_copy(low, low_buf.at[jp], local_sem.at[2])
    own_low.start()
    dip_copy = pltpu.make_async_copy(dip, d_buf, local_sem.at[3])
    dip_copy.start()
    local_1 = local_part(1)
    gathered[1][128] = jnp.zeros((BLK, LANES), jnp.bfloat16)
    cols_copy.wait()
    list_late()
    by_place(
        [(from_two, 0, 1), (low_across, 0), (from_y, 0, 0), (from_z, 0, 3), (low_across, 1), (low_across, 2), (from_y, 0, 1), (from_far, 0, 0),
         (from_y, 0, 2), (own_y, 1), (own_z, 1), (low_across, 3), (low_onward, 0), (from_far, 0, 1)],
        [(from_z, 0, 1), (from_y, 0, 0), (from_y, 0, 1), (from_z, 0, 2), (low_across, 0), (from_far, 0, 0), (from_z, 0, 3), (low_across, 1), (low_across, 2),
         (from_y, 0, 2), (from_far, 0, 1), (own_y, 1), (own_z, 1), (low_across, 3), (low_onward, 0)],
    )
    own_low.wait()
    low_arrive(zh)
    low_turn(zh)
    by_place(
        [(from_y, 0, 3), (low_onward, 1), (from_far, 0, 2), (from_two, 1, 1), (from_far, 0, 3)],
        [(from_y, 0, 3), (low_onward, 1), (from_far, 0, 2), (from_z, 1, 1), (from_far, 0, 3)],
    )
    from_sibling(0, False)
    local_0.wait()
    dip_copy.wait()
    by_place([(from_y, 1, 0), (low_onward, 2), (from_z, 1, 3)], [(from_y, 1, 0), (low_onward, 2), (from_z, 1, 2)])
    apply_rows(0, 0, 2)
    by_place([(from_y, 1, 1)], [(from_y, 1, 1)])
    apply_rows(0, 2, 2)
    tile_half(zh)
    by_place([(from_far, 1, 0)], [(from_z, 1, 3), (from_far, 1, 0)])
    low_onward(3, None)
    by_place([(from_y, 1, 2)], [(from_y, 1, 2)])
    by_place([(from_far, 1, 1)], [(from_far, 1, 1)])
    low_arrive(1 - zh)
    low_turn(1 - zh)
    by_place([(from_y, 1, 3)], [(from_y, 1, 3)])
    tile_half(1 - zh)
    sib_whole().start()
    from_sibling(1, False)
    local_1.wait()
    apply_rows(1, 0, 2)
    y_whole_fill()
    y_whole_start()
    by_place([(from_far, 1, 2)], [(from_far, 1, 2)])
    apply_rows(1, 2, 2)
    by_place([(from_far, 1, 3)], [(from_far, 1, 3)])
    from_sibling(1, True)
    apply_late()
    tile_quarters(1, 0, 3)
    y_quarter(1, 0)
    y_quarter(1, 1)
    y_quarter(1, 2)
    tile_quarters(1, 3, 1)
    y_quarter(1, 3)
    y_whole_wait()
    mine_0 = [z_quarter(0, i) for i in range(4)][3]
    z_quarter(1, 0)
    z_quarter(1, 1)
    z_quarter(1, 2)
    mine_1 = z_quarter(1, 3)
    sum_end(0, mine_0)
    for (h, key), (n, cond) in waits.items():
        slot = slots[(h, key)]
        if h == "low":
            ref = low_buf.at[0, pl.ds(0, 256)]
            copy = remote(ref, ref, send_low.at[slot], recv_low.at[0, 0], sibling)
        else:
            ref = gathered[h].at[pl.ds(0, n)]
            copy = remote(ref, ref, send_g.at[h, slot], recv_g.at[h, 0, 0], sibling)
        if cond is None:
            copy.wait_send()
        else:
            pl.when(cond)(copy.wait_send)
    sum_end(1, mine_1)


def shards(psi_low, psi_high, dip_blocks, block_cols):
    any_space = pl.BlockSpec(memory_space=pl.ANY)
    return pl.pallas_call(
        kernel,
        out_shape=pltpu.VMEM((64, 256), jnp.float32),
        in_specs=[any_space] * 4,
        out_specs=pl.BlockSpec(memory_space=pltpu.VMEM),
        scratch_shapes=[
            pltpu.VMEM((128, BLK, LANES), jnp.bfloat16),
            pltpu.VMEM((129, BLK, LANES), jnp.bfloat16),
            pltpu.VMEM((64, BLK, BLK), jnp.bfloat16),
            pltpu.VMEM((8, 1024, 256), jnp.bfloat16),
            pltpu.VMEM((2048, 1024), jnp.bfloat16),
            pltpu.VMEM((2, 1024, LANES), jnp.bfloat16),
            pltpu.VMEM((16, 2, 64, LANES), jnp.float32),
            pltpu.VMEM((16, 2, 64, LANES), jnp.float32),
            pltpu.VMEM((2, 16, 64, LANES), jnp.float32),
            pltpu.VMEM((2, 4, 4, 64, LANES), Y_TYPE),
            pltpu.VMEM((2, 4, 4, 64, LANES), Y_TYPE),
            pltpu.VMEM((2, 4, 64, LANES), Z_TYPE),
            pltpu.VMEM((2, 4, 64, LANES), Z_TYPE),
            pltpu.SemaphoreType.DMA((2, 32, 3)),
            pltpu.SemaphoreType.DMA((2, 72)),
            pltpu.SemaphoreType.DMA((8, 4)),
            pltpu.SemaphoreType.DMA((32,)),
            pltpu.SemaphoreType.DMA((2, 20)),
            pltpu.SemaphoreType.DMA((2, 20)),
            pltpu.SemaphoreType.DMA((5,)),
            pltpu.SMEM((2048,), jnp.int32),
            pltpu.VMEM((LATE, BLK, LANES), jnp.bfloat16),
            pltpu.VMEM((1024, LANES), jnp.float32),
            pltpu.VMEM((LATE + 1, BLK, LANES), jnp.float32),
            pltpu.SMEM((LATE + 5,), jnp.int32),
            pltpu.SemaphoreType.REGULAR,
        ],
        compiler_params=pltpu.CompilerParams(
            collective_id=0, has_side_effects=True, vmem_limit_bytes=56 * 1024 * 1024
        ),
        cost_estimate=pl.CostEstimate(flops=3 * 2**30, bytes_accessed=10 * 2**20, transcendentals=0),
    )(block_cols, psi_low, psi_high.reshape(4, BLK, 256), dip_blocks)


def solution(mesh):
    placed = (P("rows", "jpair"), P("rows", "jpair"), P("rows", None, None), P())
    return jax.shard_map(
        shards, mesh=mesh, in_specs=placed, out_specs=P("rows", "jpair"), check_vma=False
    )
```

```python
import functools

import jax
import jax.numpy as jnp
from jax import lax
from jax.experimental import pallas as pl
from jax.experimental.pallas import tpu as pltpu
from jax.sharding import PartitionSpec as P

BLK = 256
LANES = 128
MESH = pl.DeviceIdType.MESH
RING = 4
GROUP = 4
LATE = 16
Y_TYPE = jnp.bfloat16
Z_TYPE = jnp.bfloat16


def kernel(
    cols_all, low, high, dip, out,
    g_a, g_b, d_buf, low_buf, low_t, applied, tile_a, tile_b, sib_buf, y_send, y_recv, z_send, z_recv,
    recv_g, send_g, recv_low, send_low, recv_sum, send_sum, local_sem, cols,
    g_late, early, late_parts, late_list, across_here,
):
    gathered = (g_a, g_b)
    tiles = (tile_a, tile_b)
    jp = lax.axis_index("jpair")
    rw = lax.axis_index("rows")
    x, zh = lax.rem(jp, RING), lax.div(jp, RING)
    c, y, z = lax.rem(rw, 2), lax.rem(lax.div(rw, 2), RING), lax.div(rw, 2 * RING)

    def rows_of(zs, ys, cs):
        return (zs * RING + ys) * 2 + cs

    def ring(v, step):
        return lax.rem(v + step + RING, RING)

    def at_rows(zs, ys, cs):
        return (jp, rows_of(zs, ys, cs))

    def at_jpair(zhs, xs):
        return (zhs * RING + xs, rw)

    right, left = at_rows(z, ring(y, 1), c), at_rows(z, ring(y, -1), c)
    sibling = at_rows(z, y, 1 - c)
    y_others = [at_rows(z, ring(y, d), c) for d in (1, 2, 3)]
    z_others = [at_rows(ring(z, d), y, c) for d in (1, 2, 3)]
    x_others = [at_jpair(zh, ring(x, d)) for d in (1, 2, 3)]
    across = at_jpair(1 - zh, x)

    barrier = pltpu.get_barrier_semaphore()
    partners = [y_others[0], y_others[2], z_others[0], z_others[2], sibling, y_others[1], z_others[1]] + x_others
    for partner in partners:
        pl.semaphore_signal(barrier, inc=1, device_id=partner, device_id_type=MESH)

    @pl.when(zh == 0)
    def _():
        pl.semaphore_signal(barrier, inc=1, device_id=across, device_id_type=MESH)
        pl.semaphore_wait(barrier, len(partners))

    @pl.when(zh == 1)
    def _():
        pl.semaphore_wait(barrier, len(partners) + 1)
        pl.semaphore_signal(across_here, inc=1, device_id=across, device_id_type=MESH)

    waits = {}

    def remote(src, dst, send_sem, recv_sem, target):
        return pltpu.make_async_remote_copy(
            src_ref=src, dst_ref=dst, send_sem=send_sem, recv_sem=recv_sem,
            device_id=target, device_id_type=MESH,
        )

    inner = jnp.logical_and(z > 0, z < RING - 1)
    slots = {}

    def piece(h, r, half, n=1):
        return gathered[h].at[pl.ds(r * 4 + 2 * half, 2 * n)]

    def is_late(h, g):
        return h == 1 and g >= 2

    def late_piece(g, core, half, n=1):
        return g_late.at[pl.ds(((g - 2) * 2 + core) * 4 + 2 * half, 2 * n)]

    def send(key, h, r, half, target, src=None, n=1, cond=None, dst=None):
        dst = piece(h, r, half, n) if dst is None else dst
        sem = send_g.at[h, slots.setdefault((h, key), sum(k[0] == h for k in slots))]
        copy = remote(dst if src is None else src, dst, sem, recv_g.at[h, r, half], target)
        copy.start()
        waits[(h, key)] = (int(2 * n), cond)

    def arrive(h, r, half, n=1, ref=None):
        ref = piece(h, r, half, n) if ref is None else ref
        remote(ref, ref, send_g.at[h, 0], recv_g.at[h, r, half], sibling).wait_recv()

    def own_part(h, half, n=1):
        return high.at[pl.ds(2 * half, 2 * n), :, pl.ds(LANES * h, LANES)]

    onward = at_rows(jnp.where(z == RING - 1, z - 1, z + 1), y, c)
    downward = at_rows(ring(z, -1), y, c)
    sources = [z, z + 1 - 2 * lax.rem(z, 2), jnp.where(z < 2, 2, 1), jnp.where(z < 2, 3, 0)]

    def own_z(h, is_inner):
        for half in (0, 1):
            send(("own_z", half, 0), h, rw, half, onward, own_part(h, half))
            if is_inner:
                send(("own_z", half, 1), h, rw, half, downward, own_part(h, half), cond=inner)

    def own_y(h, is_inner):
        for half in (0, 1):
            send(("own_y", half, 0), h, rw, half, right, own_part(h, half))
            send(("own_y", 1 - half, 1), h, rw, 1 - half, left, own_part(h, 1 - half))
        send(("own_s",), h, rw, 0, sibling, own_part(h, 0, 2), n=2)

    def from_z(h, g, is_inner, halves=(0, 1)):
        zs = sources[g]
        r = rows_of(zs, y, c)
        target = at_rows(jnp.where(zs < z, lax.rem(z + 1, RING), ring(z, -1)), y, c)
        for half in halves:
            arrive(h, r, half)
            if is_inner:
                send(("z_z", g, half), h, r, half, target, cond=inner)
            send(("z_y", g, half, 0), h, r, half, right)
            send(("z_y", g, half, 1), h, r, half, left)
        if 1 in halves:
            send(("z_s", g), h, r, 0, sibling, n=2)

    def from_two(h, g, is_inner):
        for half in (0, 1):
            from_z(h, g, is_inner, (half,))
            from_z(h, g + 1, is_inner, (half,))

    def from_y(h, g, is_inner):
        r_left = rows_of(sources[g], ring(y, -1), c)
        r_right = rows_of(sources[g], ring(y, 1), c)
        arrive(h, r_left, 0)
        forward(("y_y", g, 0), h, g, r_left, 0, right)
        arrive(h, r_right, 1)
        forward(("y_y", g, 1), h, g, r_right, 1, left)
        arrive(h, r_left, 1)
        send(("y_s", g, 0), h, r_left, 0, sibling, n=2)
        arrive(h, r_right, 0)
        send(("y_s", g, 1), h, r_right, 0, sibling, n=2)

    def by_z(h, g):
        return g == 1 and h == 1

    partner = at_rows(z + 1 - 2 * lax.rem(z, 2), y, c)

    def part_of(h, r, k, n):
        return gathered[h].at[pl.ds(r * 4 + k, n)]

    def forward(key, h, g, r, half, target):
        src = piece(h, r, half) if not by_z(h, g) else part_of(h, r, 3 * half, 1)
        dst = late_piece(g, c, half) if is_late(h, g) else src
        send(key, h, r, half, target, src=src, dst=dst, n=0.5 if by_z(h, g) else 1)

    def from_far(h, g, is_inner):
        r = rows_of(sources[g], ring(y, 2), c)
        for half in (0, 1):
            ref = late_piece(g, c, half) if is_late(h, g) else None
            arrive(h, r, half, ref=part_of(h, r, 3 * half, 1) if by_z(h, g) else ref)
        middle = part_of(h, r, 1, 2)
        if g == 0 and by_z(h, 1):
            send(("f_z",), h, r, 2, partner, src=middle, dst=middle)
        if by_z(h, g):
            arrive(h, r, 2, ref=middle)
        whole = late_piece(g, c, 0, 2) if is_late(h, g) else None
        send(("f_s", g), h, r, 0, sibling, n=2, src=whole, dst=whole)

    def from_sibling(h, late):
        for g in range(RING):
            for d in range(RING):
                if late != (is_late(h, g) and d == 2):
                    continue
                ref = late_piece(g, 1 - c, 0, 2) if late else None
                arrive(h, rows_of(sources[g], ring(y, d), 1 - c), 0, 2, ref)

    def local_part(h):
        copy = pltpu.make_async_copy(
            high.at[:, :, pl.ds(LANES * h, LANES)], gathered[h].at[pl.ds(rw * 4, 4)], local_sem.at[h]
        )
        copy.start()
        return copy

    def by_place(inner_steps, end_steps):
        for is_inner, steps in ((True, inner_steps), (False, end_steps)):

            @pl.when(inner if is_inner else jnp.logical_not(inner))
            def _(is_inner=is_inner, steps=steps):
                for step in steps:
                    step[0](*step[1:], is_inner)

    LOW_PARTS = 4

    def send_low_to(key, j, target, src, part):
        dst = low_buf.at[j, pl.ds(part * 256, 256)]
        if src is None:
            src = dst
        sem = send_low.at[slots.setdefault(("low", key), sum(k[0] == "low" for k in slots))]
        copy = remote(src, dst, sem, recv_low.at[j, part], target)
        copy.start()
        waits[("low", key)] = (0, None)

    def arrive_low(j, part):
        dst = low_buf.at[j, pl.ds(part * 256, 256)]
        remote(dst, dst, send_low.at[0], recv_low.at[j, part], sibling).wait_recv()

    j_across = (1 - zh) * RING + x

    def low_x(is_inner):
        for part in range(LOW_PARTS):
            for d in range(3):
                send_low_to(("x", d, part), jp, x_others[d], low.at[pl.ds(part * 256, 256)], part)

    def low_across(part, is_inner):
        if part == 0:

            @pl.when(zh == 0)
            def _():
                pl.semaphore_wait(across_here, 1)

        send_low_to(("across", part), jp, across, low.at[pl.ds(part * 256, 256)], part)

    def low_onward(part, is_inner):
        arrive_low(j_across, part)
        for d in range(3):
            send_low_to(("onward", d, part), j_across, x_others[d], None, part)

    def low_arrive(zhs):
        for part in range(LOW_PARTS):
            for d in (1, 2, 3):
                arrive_low(zhs * RING + ring(x, d), part)

    def low_turn(zhs):
        def one(i, _):
            j = zhs * RING + i
            low_t[pl.ds(pl.multiple_of(j * BLK, BLK), BLK), :] = low_buf[j].T
            return 0

        lax.fori_loop(0, RING, one, 0)

    def place_of(b):
        col = cols[rw * 64 + b]
        chip = lax.shift_right_logical(col, 3)
        late_2 = chip == sources[2] * RING + ring(y, 2)
        late_3 = chip == sources[3] * RING + ring(y, 2)
        return col, jnp.logical_or(late_2, late_3), jnp.bitwise_and(col, 7) + 8 * late_3.astype(jnp.int32)

    def block_of(h, b):
        col, late, _ = place_of(b)
        return gathered[h][col if h == 0 else jnp.where(late, 128, col)]

    def apply_rows(h, q0, n):
        def row(q, _):
            def some(i, total):
                b = q * 16 + i * GROUP
                lhs = jnp.concatenate([d_buf[b + k] for k in range(GROUP)], axis=1)
                rhs = jnp.concatenate([block_of(h, b + k) for k in range(GROUP)], axis=0)
                return total + jnp.dot(lhs, rhs, preferred_element_type=jnp.float32)

            total = lax.fori_loop(0, 16 // GROUP, some, jnp.zeros((BLK, LANES), jnp.float32))
            here = pl.ds(pl.multiple_of(q * BLK, BLK), BLK)
            if h == 0:
                applied[h, here, :] = total.astype(jnp.bfloat16)
            else:
                early[here, :] = total
            return 0

        lax.fori_loop(q0, q0 + n, row, 0)

    def list_late():
        def one(b, carry):
            count, found = carry[0], carry[1:]
            _, late, _ = place_of(b)
            found = tuple(jnp.where(jnp.logical_and(late, count == i), b, f) for i, f in enumerate(found))
            return (count + late.astype(jnp.int32),) + found

        carry = (jnp.int32(0),) + (jnp.int32(0),) * LATE
        for q in range(4):
            late_list[LATE + q] = jnp.minimum(carry[0], LATE)
            carry = lax.fori_loop(16 * q, 16 * q + 16, one, carry)
        late_list[LATE + 4] = jnp.minimum(carry[0], LATE)
        for i in range(LATE):
            late_list[i] = carry[1 + i]

    def apply_late():
        late_parts[0] = jnp.zeros((BLK, LANES), jnp.float32)

        def one(i, total):
            for k in range(4):
                b = jnp.bitwise_and(late_list[4 * i + k], 63)
                _, _, at = place_of(b)
                total = total + jnp.dot(d_buf[b], g_late[at], preferred_element_type=jnp.float32)
                late_parts[4 * i + k + 1] = total
            return total

        lax.fori_loop(0, LATE // 4, one, jnp.zeros((BLK, LANES), jnp.float32))
        for q in range(4):
            here = pl.ds(q * BLK, BLK)
            first, last = (jnp.clip(late_list[LATE + q + k], 0, LATE) for k in (0, 1))
            total = early[here, :] + (late_parts[last] - late_parts[first])
            applied[1, here, :] = total.astype(jnp.bfloat16)

    quarters = [3 - z, jnp.where(z < 2, z + 2, z - 2), z + 1 - 2 * lax.rem(z, 2), z]

    def sum_copy(h, k, src, dst, target):
        return remote(src, dst, send_sum.at[h, k], recv_sum.at[h, k], target)

    def sib_copy(h, i):
        part = pl.ds(4 * quarters[i], 4)
        return sum_copy(h, i, tiles[h].at[part, 1 - c], sib_buf.at[h, part], sibling)

    def y_copy(h, i, d):
        return sum_copy(h, 3 + 3 * i + d, y_send.at[h, d, i], y_recv.at[h, d, i], y_others[d - 1])

    def z_copy(h, i):
        return sum_copy(h, 16 + i, z_send.at[h, i], z_recv.at[h, i], at_rows(quarters[i], y, c))

    def tile_quarters(h, i0, n, first=None):
        def one(i, _):
            quarter = first + i if h == 0 else jnp.where(i < 2, jnp.where(i == 0, quarters[0], quarters[1]), jnp.where(i == 2, quarters[2], z))
            rows = pl.ds(pl.multiple_of(quarter * 512, 512), 512)
            part = jnp.dot(low_t[rows, :], applied[h], preferred_element_type=jnp.float32)
            tiles[h][pl.ds(4 * quarter, 4)] = part.reshape(4, 2, 64, LANES)
            if h == 1:
                at = pl.ds(4 * quarter, 4)
                sum_copy(h, i, tiles[h].at[at, 1 - c], sib_buf.at[h, at], sibling).start()
            return 0

        lax.fori_loop(i0, i0 + n, one, 0)

    def y_quarter(h, i):
        sib_copy(h, i).wait()
        for d in (2, 1, 3):
            p = quarters[i] * 4 + ring(y, d)
            y_send[h, d, i] = (tiles[h][p, c] + sib_buf[h, p]).astype(Y_TYPE)
            y_copy(h, i, d).start()

    def z_quarter(h, i):
        if h == 1:
            for d in (1, 2, 3):
                y_copy(h, i, d).wait()
        p = quarters[i] * 4 + y
        total = tiles[h][p, c] + sib_buf[h, p]
        for d in (1, 2, 3):
            total = total + y_recv[h, d, i].astype(jnp.float32)
        if i == 3:
            return total
        z_send[h, i] = total.astype(Z_TYPE)
        z_copy(h, i).start()

    def sib_whole():
        return sum_copy(0, 0, tiles[0].at[:, 1 - c], sib_buf.at[0], sibling)

    def y_whole(d):
        return sum_copy(0, 3 + d, y_send.at[0, d], y_recv.at[0, d], y_others[d - 1])

    def tile_half(zhs):
        tile_quarters(0, 0, 2, 2 * zhs)

    def y_whole_fill():
        sib_whole().wait()
        for d in (2, 1, 3):
            for i in range(4):
                p = quarters[i] * 4 + ring(y, d)
                y_send[0, d, i] = (tiles[0][p, c] + sib_buf[0, p]).astype(Y_TYPE)

    def y_whole_start():
        for d in (2, 1, 3):
            y_whole(d).start()

    def y_whole_wait():
        for d in (2, 1, 3):
            y_whole(d).wait()

    def sum_end(h, total):
        for i in range(3):
            z_copy(h, i).wait()
            total = total + z_recv[h, i].astype(jnp.float32)
        out[:, LANES * h : LANES * (h + 1)] = total

    cols_copy = pltpu.make_async_copy(cols_all, cols, local_sem.at[4])
    cols_copy.start()
    by_place([(own_z, 0), (own_y, 0)], [(own_z, 0), (own_y, 0)])
    local_0 = local_part(0)
    low_x(None)
    own_low = pltpu.make_async_copy(low, low_buf.at[jp], local_sem.at[2])
    own_low.start()
    dip_copy = pltpu.make_async_copy(dip, d_buf, local_sem.at[3])
    dip_copy.start()
    local_1 = local_part(1)
    gathered[1][128] = jnp.zeros((BLK, LANES), jnp.bfloat16)
    cols_copy.wait()
    list_late()
    by_place(
        [(from_two, 0, 1), (low_across, 0), (from_y, 0, 0), (from_z, 0, 3), (low_across, 1), (low_across, 2), (from_y, 0, 1), (from_far, 0, 0),
         (from_y, 0, 2), (own_y, 1), (own_z, 1), (low_across, 3), (low_onward, 0), (from_far, 0, 1)],
        [(from_z, 0, 1), (from_y, 0, 0), (from_y, 0, 1), (from_z, 0, 2), (low_across, 0), (from_far, 0, 0), (from_z, 0, 3), (low_across, 1), (low_across, 2),
         (from_y, 0, 2), (from_far, 0, 1), (own_y, 1), (own_z, 1), (low_across, 3), (low_onward, 0)],
    )
    own_low.wait()
    low_arrive(zh)
    low_turn(zh)
    by_place(
        [(from_y, 0, 3), (low_onward, 1), (from_far, 0, 2), (from_two, 1, 1), (from_far, 0, 3)],
        [(from_y, 0, 3), (low_onward, 1), (from_far, 0, 2), (from_z, 1, 1), (from_far, 0, 3)],
    )
    from_sibling(0, False)
    local_0.wait()
    dip_copy.wait()
    by_place([(from_y, 1, 0), (low_onward, 2)], [(from_y, 1, 0), (low_onward, 2)])
    apply_rows(0, 0, 2)
    by_place([(from_y, 1, 1), (from_z, 1, 3)], [(from_y, 1, 1), (from_z, 1, 2)])
    apply_rows(0, 2, 2)
    tile_half(zh)
    by_place([(from_far, 1, 0)], [(from_z, 1, 3), (from_far, 1, 0)])
    low_onward(3, None)
    by_place([(from_y, 1, 2)], [(from_y, 1, 2)])
    by_place([(from_far, 1, 1)], [(from_far, 1, 1)])
    low_arrive(1 - zh)
    low_turn(1 - zh)
    by_place([(from_y, 1, 3)], [(from_y, 1, 3)])
    tile_half(1 - zh)
    sib_whole().start()
    from_sibling(1, False)
    local_1.wait()
    apply_rows(1, 0, 2)
    y_whole_fill()
    y_whole_start()
    by_place([(from_far, 1, 2)], [(from_far, 1, 2)])
    apply_rows(1, 2, 2)
    by_place([(from_far, 1, 3)], [(from_far, 1, 3)])
    from_sibling(1, True)
    apply_late()
    tile_quarters(1, 0, 3)
    y_quarter(1, 0)
    y_quarter(1, 1)
    y_quarter(1, 2)
    tile_quarters(1, 3, 1)
    y_quarter(1, 3)
    y_whole_wait()
    mine_0 = [z_quarter(0, i) for i in range(4)][3]
    z_quarter(1, 0)
    z_quarter(1, 1)
    z_quarter(1, 2)
    mine_1 = z_quarter(1, 3)
    sum_end(0, mine_0)
    for (h, key), (n, cond) in waits.items():
        slot = slots[(h, key)]
        if h == "low":
            ref = low_buf.at[0, pl.ds(0, 256)]
            copy = remote(ref, ref, send_low.at[slot], recv_low.at[0, 0], sibling)
        else:
            ref = gathered[h].at[pl.ds(0, n)]
            copy = remote(ref, ref, send_g.at[h, slot], recv_g.at[h, 0, 0], sibling)
        if cond is None:
            copy.wait_send()
        else:
            pl.when(cond)(copy.wait_send)
    sum_end(1, mine_1)


def shards(psi_low, psi_high, dip_blocks, block_cols):
    any_space = pl.BlockSpec(memory_space=pl.ANY)
    return pl.pallas_call(
        kernel,
        out_shape=pltpu.VMEM((64, 256), jnp.float32),
        in_specs=[any_space] * 4,
        out_specs=pl.BlockSpec(memory_space=pltpu.VMEM),
        scratch_shapes=[
            pltpu.VMEM((128, BLK, LANES), jnp.bfloat16),
            pltpu.VMEM((129, BLK, LANES), jnp.bfloat16),
            pltpu.VMEM((64, BLK, BLK), jnp.bfloat16),
            pltpu.VMEM((8, 1024, 256), jnp.bfloat16),
            pltpu.VMEM((2048, 1024), jnp.bfloat16),
            pltpu.VMEM((2, 1024, LANES), jnp.bfloat16),
            pltpu.VMEM((16, 2, 64, LANES), jnp.float32),
            pltpu.VMEM((16, 2, 64, LANES), jnp.float32),
            pltpu.VMEM((2, 16, 64, LANES), jnp.float32),
            pltpu.VMEM((2, 4, 4, 64, LANES), Y_TYPE),
            pltpu.VMEM((2, 4, 4, 64, LANES), Y_TYPE),
            pltpu.VMEM((2, 4, 64, LANES), Z_TYPE),
            pltpu.VMEM((2, 4, 64, LANES), Z_TYPE),
            pltpu.SemaphoreType.DMA((2, 32, 3)),
            pltpu.SemaphoreType.DMA((2, 72)),
            pltpu.SemaphoreType.DMA((8, 4)),
            pltpu.SemaphoreType.DMA((32,)),
            pltpu.SemaphoreType.DMA((2, 20)),
            pltpu.SemaphoreType.DMA((2, 20)),
            pltpu.SemaphoreType.DMA((5,)),
            pltpu.SMEM((2048,), jnp.int32),
            pltpu.VMEM((LATE, BLK, LANES), jnp.bfloat16),
            pltpu.VMEM((1024, LANES), jnp.float32),
            pltpu.VMEM((LATE + 1, BLK, LANES), jnp.float32),
            pltpu.SMEM((LATE + 5,), jnp.int32),
            pltpu.SemaphoreType.REGULAR,
        ],
        compiler_params=pltpu.CompilerParams(
            collective_id=0, has_side_effects=True, vmem_limit_bytes=56 * 1024 * 1024
        ),
        cost_estimate=pl.CostEstimate(flops=3 * 2**30, bytes_accessed=10 * 2**20, transcendentals=0),
    )(block_cols, psi_low, psi_high.reshape(4, BLK, 256), dip_blocks)


def solution(mesh):
    placed = (P("rows", "jpair"), P("rows", "jpair"), P("rows", None, None), P())
    return jax.shard_map(
        shards, mesh=mesh, in_specs=placed, out_specs=P("rows", "jpair"), check_vma=False
    )
```

```python
import functools

import jax
import jax.numpy as jnp
from jax import lax
from jax.experimental import pallas as pl
from jax.experimental.pallas import tpu as pltpu
from jax.sharding import PartitionSpec as P

BLK = 256
LANES = 128
MESH = pl.DeviceIdType.MESH
RING = 4
GROUP = 4
LATE = 16
Y_TYPE = jnp.bfloat16
Z_TYPE = jnp.bfloat16


def kernel(
    cols_all, low, high, dip, out,
    g_a, g_b, d_buf, low_buf, low_t, applied, tile_a, tile_b, sib_buf, y_send, y_recv, z_send, z_recv,
    recv_g, send_g, recv_low, send_low, recv_sum, send_sum, local_sem, cols,
    g_late, early, late_parts, late_list, across_here, higher_here,
):
    gathered = (g_a, g_b)
    tiles = (tile_a, tile_b)
    jp = lax.axis_index("jpair")
    rw = lax.axis_index("rows")
    x, zh = lax.rem(jp, RING), lax.div(jp, RING)
    c, y, z = lax.rem(rw, 2), lax.rem(lax.div(rw, 2), RING), lax.div(rw, 2 * RING)

    def rows_of(zs, ys, cs):
        return (zs * RING + ys) * 2 + cs

    def ring(v, step):
        return lax.rem(v + step + RING, RING)

    def at_rows(zs, ys, cs):
        return (jp, rows_of(zs, ys, cs))

    def at_jpair(zhs, xs):
        return (zhs * RING + xs, rw)

    right, left = at_rows(z, ring(y, 1), c), at_rows(z, ring(y, -1), c)
    sibling = at_rows(z, y, 1 - c)
    y_others = [at_rows(z, ring(y, d), c) for d in (1, 2, 3)]
    z_others = [at_rows(ring(z, d), y, c) for d in (1, 2, 3)]
    x_others = [at_jpair(zh, ring(x, d)) for d in (1, 2, 3)]
    across = at_jpair(1 - zh, x)

    barrier = pltpu.get_barrier_semaphore()
    partners = [y_others[0], y_others[2], sibling, y_others[1]] + x_others
    for partner in partners:
        pl.semaphore_signal(barrier, inc=1, device_id=partner, device_id_type=MESH)

    for zs in range(1, RING):

        @pl.when(zs > z)
        def _(zs=zs):
            pl.semaphore_signal(barrier, inc=1, device_id=at_rows(zs, y, c), device_id_type=MESH)

    @pl.when(zh == 0)
    def _():
        pl.semaphore_signal(barrier, inc=1, device_id=across, device_id_type=MESH)
        pl.semaphore_wait(barrier, len(partners) + z)

    @pl.when(zh == 1)
    def _():
        pl.semaphore_wait(barrier, len(partners) + 1 + z)
        pl.semaphore_signal(across_here, inc=1, device_id=across, device_id_type=MESH)

    for zs in range(RING - 1):

        @pl.when(zs < z)
        def _(zs=zs):
            pl.semaphore_signal(higher_here.at[z], inc=1, device_id=at_rows(zs, y, c), device_id_type=MESH)

    def wait_higher(first, last):
        for zs in range(1, RING):

            @pl.when(jnp.logical_and(zs >= z + first, zs <= z + last))
            def _(zs=zs):
                pl.semaphore_wait(higher_here.at[zs], 1)

    waits = {}

    def remote(src, dst, send_sem, recv_sem, target):
        return pltpu.make_async_remote_copy(
            src_ref=src, dst_ref=dst, send_sem=send_sem, recv_sem=recv_sem,
            device_id=target, device_id_type=MESH,
        )

    inner = jnp.logical_and(z > 0, z < RING - 1)
    slots = {}

    def piece(h, r, half, n=1):
        return gathered[h].at[pl.ds(r * 4 + 2 * half, 2 * n)]

    def is_late(h, g):
        return h == 1 and g >= 2

    def late_piece(g, core, half, n=1):
        return g_late.at[pl.ds(((g - 2) * 2 + core) * 4 + 2 * half, 2 * n)]

    def send(key, h, r, half, target, src=None, n=1, cond=None, dst=None):
        dst = piece(h, r, half, n) if dst is None else dst
        sem = send_g.at[h, slots.setdefault((h, key), sum(k[0] == h for k in slots))]
        copy = remote(dst if src is None else src, dst, sem, recv_g.at[h, r, half], target)
        copy.start()
        waits[(h, key)] = (int(2 * n), cond)

    def arrive(h, r, half, n=1, ref=None):
        ref = piece(h, r, half, n) if ref is None else ref
        remote(ref, ref, send_g.at[h, 0], recv_g.at[h, r, half], sibling).wait_recv()

    def own_part(h, half, n=1):
        return high.at[pl.ds(2 * half, 2 * n), :, pl.ds(LANES * h, LANES)]

    onward = at_rows(jnp.where(z == RING - 1, z - 1, z + 1), y, c)
    downward = at_rows(ring(z, -1), y, c)
    sources = [z, z + 1 - 2 * lax.rem(z, 2), jnp.where(z < 2, 2, 1), jnp.where(z < 2, 3, 0)]

    def own_z(h, is_inner):
        for half in (0, 1):
            send(("own_z", half, 0), h, rw, half, onward, own_part(h, half))
            if is_inner:
                send(("own_z", half, 1), h, rw, half, downward, own_part(h, half), cond=inner)

    def own_y(h, is_inner):
        for half in (0, 1):
            send(("own_y", half, 0), h, rw, half, right, own_part(h, half))
            send(("own_y", 1 - half, 1), h, rw, 1 - half, left, own_part(h, 1 - half))
        send(("own_s",), h, rw, 0, sibling, own_part(h, 0, 2), n=2)

    def from_z(h, g, is_inner, halves=(0, 1)):
        zs = sources[g]
        r = rows_of(zs, y, c)
        target = at_rows(jnp.where(zs < z, lax.rem(z + 1, RING), ring(z, -1)), y, c)
        for half in halves:
            arrive(h, r, half)
            if is_inner:
                send(("z_z", g, half), h, r, half, target, cond=inner)
            send(("z_y", g, half, 0), h, r, half, right)
            send(("z_y", g, half, 1), h, r, half, left)
        if 1 in halves:
            send(("z_s", g), h, r, 0, sibling, n=2)

    def from_two(h, g, is_inner):
        for half in (0, 1):
            from_z(h, g, is_inner, (half,))
            from_z(h, g + 1, is_inner, (half,))

    def from_y(h, g, is_inner):
        r_left = rows_of(sources[g], ring(y, -1), c)
        r_right = rows_of(sources[g], ring(y, 1), c)
        arrive(h, r_left, 0)
        forward(("y_y", g, 0), h, g, r_left, 0, right)
        arrive(h, r_right, 1)
        forward(("y_y", g, 1), h, g, r_right, 1, left)
        arrive(h, r_left, 1)
        send(("y_s", g, 0), h, r_left, 0, sibling, n=2)
        arrive(h, r_right, 0)
        send(("y_s", g, 1), h, r_right, 0, sibling, n=2)

    def by_z(h, g):
        return g == 1 and h == 1

    partner = at_rows(z + 1 - 2 * lax.rem(z, 2), y, c)

    def part_of(h, r, k, n):
        return gathered[h].at[pl.ds(r * 4 + k, n)]

    def forward(key, h, g, r, half, target):
        src = piece(h, r, half) if not by_z(h, g) else part_of(h, r, 3 * half, 1)
        dst = late_piece(g, c, half) if is_late(h, g) else src
        send(key, h, r, half, target, src=src, dst=dst, n=0.5 if by_z(h, g) else 1)

    def from_far(h, g, is_inner):
        r = rows_of(sources[g], ring(y, 2), c)
        for half in (0, 1):
            ref = late_piece(g, c, half) if is_late(h, g) else None
            arrive(h, r, half, ref=part_of(h, r, 3 * half, 1) if by_z(h, g) else ref)
        middle = part_of(h, r, 1, 2)
        if g == 0 and by_z(h, 1):
            send(("f_z",), h, r, 2, partner, src=middle, dst=middle)
        if by_z(h, g):
            arrive(h, r, 2, ref=middle)
        whole = late_piece(g, c, 0, 2) if is_late(h, g) else None
        send(("f_s", g), h, r, 0, sibling, n=2, src=whole, dst=whole)

    def from_sibling(h, late):
        for g in range(RING):
            for d in range(RING):
                if late != (is_late(h, g) and d == 2):
                    continue
                ref = late_piece(g, 1 - c, 0, 2) if late else None
                arrive(h, rows_of(sources[g], ring(y, d), 1 - c), 0, 2, ref)

    def local_part(h):
        copy = pltpu.make_async_copy(
            high.at[:, :, pl.ds(LANES * h, LANES)], gathered[h].at[pl.ds(rw * 4, 4)], local_sem.at[h]
        )
        copy.start()
        return copy

    def by_place(inner_steps, end_steps):
        for is_inner, steps in ((True, inner_steps), (False, end_steps)):

            @pl.when(inner if is_inner else jnp.logical_not(inner))
            def _(is_inner=is_inner, steps=steps):
                for step in steps:
                    step[0](*step[1:], is_inner)

    LOW_PARTS = 4

    def send_low_to(key, j, target, src, part):
        dst = low_buf.at[j, pl.ds(part * 256, 256)]
        if src is None:
            src = dst
        sem = send_low.at[slots.setdefault(("low", key), sum(k[0] == "low" for k in slots))]
        copy = remote(src, dst, sem, recv_low.at[j, part], target)
        copy.start()
        waits[("low", key)] = (0, None)

    def arrive_low(j, part):
        dst = low_buf.at[j, pl.ds(part * 256, 256)]
        remote(dst, dst, send_low.at[0], recv_low.at[j, part], sibling).wait_recv()

    j_across = (1 - zh) * RING + x

    def low_x(is_inner):
        for part in range(LOW_PARTS):
            for d in range(3):
                send_low_to(("x", d, part), jp, x_others[d], low.at[pl.ds(part * 256, 256)], part)

    def low_across(part, is_inner):
        if part == 0:

            @pl.when(zh == 0)
            def _():
                pl.semaphore_wait(across_here, 1)

        send_low_to(("across", part), jp, across, low.at[pl.ds(part * 256, 256)], part)

    def low_onward(part, is_inner):
        arrive_low(j_across, part)
        for d in range(3):
            send_low_to(("onward", d, part), j_across, x_others[d], None, part)

    def low_arrive(zhs):
        for part in range(LOW_PARTS):
            for d in (1, 2, 3):
                arrive_low(zhs * RING + ring(x, d), part)

    def low_turn(zhs):
        def one(i, _):
            j = zhs * RING + i
            low_t[pl.ds(pl.multiple_of(j * BLK, BLK), BLK), :] = low_buf[j].T
            return 0

        lax.fori_loop(0, RING, one, 0)

    def place_of(b):
        col = cols[rw * 64 + b]
        chip = lax.shift_right_logical(col, 3)
        late_2 = chip == sources[2] * RING + ring(y, 2)
        late_3 = chip == sources[3] * RING + ring(y, 2)
        return col, jnp.logical_or(late_2, late_3), jnp.bitwise_and(col, 7) + 8 * late_3.astype(jnp.int32)

    def block_of(h, b):
        col, late, _ = place_of(b)
        return gathered[h][col if h == 0 else jnp.where(late, 128, col)]

    def apply_rows(h, q0, n):
        def row(q, _):
            def some(i, total):
                b = q * 16 + i * GROUP
                lhs = jnp.concatenate([d_buf[b + k] for k in range(GROUP)], axis=1)
                rhs = jnp.concatenate([block_of(h, b + k) for k in range(GROUP)], axis=0)
                return total + jnp.dot(lhs, rhs, preferred_element_type=jnp.float32)

            total = lax.fori_loop(0, 16 // GROUP, some, jnp.zeros((BLK, LANES), jnp.float32))
            here = pl.ds(pl.multiple_of(q * BLK, BLK), BLK)
            if h == 0:
                applied[h, here, :] = total.astype(jnp.bfloat16)
            else:
                early[here, :] = total
            return 0

        lax.fori_loop(q0, q0 + n, row, 0)

    def list_late():
        def one(b, carry):
            count, found = carry[0], carry[1:]
            _, late, _ = place_of(b)
            found = tuple(jnp.where(jnp.logical_and(late, count == i), b, f) for i, f in enumerate(found))
            return (count + late.astype(jnp.int32),) + found

        carry = (jnp.int32(0),) + (jnp.int32(0),) * LATE
        for q in range(4):
            late_list[LATE + q] = jnp.minimum(carry[0], LATE)
            carry = lax.fori_loop(16 * q, 16 * q + 16, one, carry)
        late_list[LATE + 4] = jnp.minimum(carry[0], LATE)
        for i in range(LATE):
            late_list[i] = carry[1 + i]

    def apply_late():
        late_parts[0] = jnp.zeros((BLK, LANES), jnp.float32)

        def one(i, total):
            for k in range(4):
                b = jnp.bitwise_and(late_list[4 * i + k], 63)
                _, _, at = place_of(b)
                total = total + jnp.dot(d_buf[b], g_late[at], preferred_element_type=jnp.float32)
                late_parts[4 * i + k + 1] = total
            return total

        lax.fori_loop(0, LATE // 4, one, jnp.zeros((BLK, LANES), jnp.float32))
        for q in range(4):
            here = pl.ds(q * BLK, BLK)
            first, last = (jnp.clip(late_list[LATE + q + k], 0, LATE) for k in (0, 1))
            total = early[here, :] + (late_parts[last] - late_parts[first])
            applied[1, here, :] = total.astype(jnp.bfloat16)

    quarters = [3 - z, jnp.where(z < 2, z + 2, z - 2), z + 1 - 2 * lax.rem(z, 2), z]

    def sum_copy(h, k, src, dst, target):
        return remote(src, dst, send_sum.at[h, k], recv_sum.at[h, k], target)

    def sib_copy(h, i):
        part = pl.ds(4 * quarters[i], 4)
        return sum_copy(h, i, tiles[h].at[part, 1 - c], sib_buf.at[h, part], sibling)

    def y_copy(h, i, d):
        return sum_copy(h, 3 + 3 * i + d, y_send.at[h, d, i], y_recv.at[h, d, i], y_others[d - 1])

    def z_copy(h, i):
        return sum_copy(h, 16 + i, z_send.at[h, i], z_recv.at[h, i], at_rows(quarters[i], y, c))

    def tile_quarters(h, i0, n, first=None):
        def one(i, _):
            quarter = first + i if h == 0 else jnp.where(i < 2, jnp.where(i == 0, quarters[0], quarters[1]), jnp.where(i == 2, quarters[2], z))
            rows = pl.ds(pl.multiple_of(quarter * 512, 512), 512)
            part = jnp.dot(low_t[rows, :], applied[h], preferred_element_type=jnp.float32)
            tiles[h][pl.ds(4 * quarter, 4)] = part.reshape(4, 2, 64, LANES)
            if h == 1:
                at = pl.ds(4 * quarter, 4)
                sum_copy(h, i, tiles[h].at[at, 1 - c], sib_buf.at[h, at], sibling).start()
            return 0

        lax.fori_loop(i0, i0 + n, one, 0)

    def y_quarter(h, i):
        sib_copy(h, i).wait()
        for d in (2, 1, 3):
            p = quarters[i] * 4 + ring(y, d)
            y_send[h, d, i] = (tiles[h][p, c] + sib_buf[h, p]).astype(Y_TYPE)
            y_copy(h, i, d).start()

    def z_quarter(h, i):
        if h == 1:
            for d in (1, 2, 3):
                y_copy(h, i, d).wait()
        p = quarters[i] * 4 + y
        total = tiles[h][p, c] + sib_buf[h, p]
        for d in (1, 2, 3):
            total = total + y_recv[h, d, i].astype(jnp.float32)
        if i == 3:
            return total
        z_send[h, i] = total.astype(Z_TYPE)
        z_copy(h, i).start()

    def sib_whole():
        return sum_copy(0, 0, tiles[0].at[:, 1 - c], sib_buf.at[0], sibling)

    def y_whole(d):
        return sum_copy(0, 3 + d, y_send.at[0, d], y_recv.at[0, d], y_others[d - 1])

    def tile_half(zhs):
        tile_quarters(0, 0, 2, 2 * zhs)

    def y_whole_fill():
        sib_whole().wait()
        for d in (2, 1, 3):
            for i in range(4):
                p = quarters[i] * 4 + ring(y, d)
                y_send[0, d, i] = (tiles[0][p, c] + sib_buf[0, p]).astype(Y_TYPE)

    def y_whole_start():
        for d in (2, 1, 3):
            y_whole(d).start()

    def y_whole_wait():
        for d in (2, 1, 3):
            y_whole(d).wait()

    def sum_end(h, total):
        for i in range(3):
            z_copy(h, i).wait()
            total = total + z_recv[h, i].astype(jnp.float32)
        out[:, LANES * h : LANES * (h + 1)] = total

    cols_copy = pltpu.make_async_copy(cols_all, cols, local_sem.at[4])
    cols_copy.start()
    by_place([(own_y, 0)], [(own_y, 0)])
    wait_higher(1, 1)
    by_place([(own_z, 0)], [(own_z, 0)])
    local_0 = local_part(0)
    low_x(None)
    own_low = pltpu.make_async_copy(low, low_buf.at[jp], local_sem.at[2])
    own_low.start()
    dip_copy = pltpu.make_async_copy(dip, d_buf, local_sem.at[3])
    dip_copy.start()
    local_1 = local_part(1)
    gathered[1][128] = jnp.zeros((BLK, LANES), jnp.bfloat16)
    cols_copy.wait()
    list_late()
    by_place(
        [(from_two, 0, 1), (low_across, 0), (from_y, 0, 0), (from_z, 0, 3), (low_across, 1), (low_across, 2), (from_y, 0, 1), (from_far, 0, 0),
         (from_y, 0, 2), (own_y, 1), (own_z, 1), (low_across, 3), (low_onward, 0), (from_far, 0, 1)],
        [(from_z, 0, 1), (from_y, 0, 0), (from_y, 0, 1), (from_z, 0, 2), (low_across, 0), (from_far, 0, 0), (from_z, 0, 3), (low_across, 1), (low_across, 2),
         (from_y, 0, 2), (from_far, 0, 1), (own_y, 1), (own_z, 1), (low_across, 3), (low_onward, 0)],
    )
    own_low.wait()
    low_arrive(zh)
    low_turn(zh)
    by_place(
        [(from_y, 0, 3), (low_onward, 1), (from_far, 0, 2), (from_two, 1, 1), (from_far, 0, 3)],
        [(from_y, 0, 3), (low_onward, 1), (from_far, 0, 2), (from_z, 1, 1), (from_far, 0, 3)],
    )
    wait_higher(2, 3)
    from_sibling(0, False)
    local_0.wait()
    dip_copy.wait()
    by_place([(from_y, 1, 0), (low_onward, 2)], [(from_y, 1, 0), (low_onward, 2)])
    apply_rows(0, 0, 2)
    by_place([(from_y, 1, 1), (from_z, 1, 3)], [(from_y, 1, 1), (from_z, 1, 2)])
    apply_rows(0, 2, 2)
    tile_half(zh)
    by_place([(from_far, 1, 0)], [(from_z, 1, 3), (from_far, 1, 0)])
    low_onward(3, None)
    by_place([(from_y, 1, 2)], [(from_y, 1, 2)])
    by_place([(from_far, 1, 1)], [(from_far, 1, 1)])
    low_arrive(1 - zh)
    low_turn(1 - zh)
    by_place([(from_y, 1, 3)], [(from_y, 1, 3)])
    tile_half(1 - zh)
    sib_whole().start()
    from_sibling(1, False)
    local_1.wait()
    apply_rows(1, 0, 2)
    y_whole_fill()
    y_whole_start()
    by_place([(from_far, 1, 2)], [(from_far, 1, 2)])
    apply_rows(1, 2, 2)
    by_place([(from_far, 1, 3)], [(from_far, 1, 3)])
    from_sibling(1, True)
    apply_late()
    tile_quarters(1, 0, 3)
    y_quarter(1, 0)
    y_quarter(1, 1)
    y_quarter(1, 2)
    tile_quarters(1, 3, 1)
    y_quarter(1, 3)
    y_whole_wait()
    mine_0 = [z_quarter(0, i) for i in range(4)][3]
    z_quarter(1, 0)
    z_quarter(1, 1)
    z_quarter(1, 2)
    mine_1 = z_quarter(1, 3)
    sum_end(0, mine_0)
    for (h, key), (n, cond) in waits.items():
        slot = slots[(h, key)]
        if h == "low":
            ref = low_buf.at[0, pl.ds(0, 256)]
            copy = remote(ref, ref, send_low.at[slot], recv_low.at[0, 0], sibling)
        else:
            ref = gathered[h].at[pl.ds(0, n)]
            copy = remote(ref, ref, send_g.at[h, slot], recv_g.at[h, 0, 0], sibling)
        if cond is None:
            copy.wait_send()
        else:
            pl.when(cond)(copy.wait_send)
    sum_end(1, mine_1)


def shards(psi_low, psi_high, dip_blocks, block_cols):
    any_space = pl.BlockSpec(memory_space=pl.ANY)
    return pl.pallas_call(
        kernel,
        out_shape=pltpu.VMEM((64, 256), jnp.float32),
        in_specs=[any_space] * 4,
        out_specs=pl.BlockSpec(memory_space=pltpu.VMEM),
        scratch_shapes=[
            pltpu.VMEM((128, BLK, LANES), jnp.bfloat16),
            pltpu.VMEM((129, BLK, LANES), jnp.bfloat16),
            pltpu.VMEM((64, BLK, BLK), jnp.bfloat16),
            pltpu.VMEM((8, 1024, 256), jnp.bfloat16),
            pltpu.VMEM((2048, 1024), jnp.bfloat16),
            pltpu.VMEM((2, 1024, LANES), jnp.bfloat16),
            pltpu.VMEM((16, 2, 64, LANES), jnp.float32),
            pltpu.VMEM((16, 2, 64, LANES), jnp.float32),
            pltpu.VMEM((2, 16, 64, LANES), jnp.float32),
            pltpu.VMEM((2, 4, 4, 64, LANES), Y_TYPE),
            pltpu.VMEM((2, 4, 4, 64, LANES), Y_TYPE),
            pltpu.VMEM((2, 4, 64, LANES), Z_TYPE),
            pltpu.VMEM((2, 4, 64, LANES), Z_TYPE),
            pltpu.SemaphoreType.DMA((2, 32, 3)),
            pltpu.SemaphoreType.DMA((2, 72)),
            pltpu.SemaphoreType.DMA((8, 4)),
            pltpu.SemaphoreType.DMA((32,)),
            pltpu.SemaphoreType.DMA((2, 20)),
            pltpu.SemaphoreType.DMA((2, 20)),
            pltpu.SemaphoreType.DMA((5,)),
            pltpu.SMEM((2048,), jnp.int32),
            pltpu.VMEM((LATE, BLK, LANES), jnp.bfloat16),
            pltpu.VMEM((1024, LANES), jnp.float32),
            pltpu.VMEM((LATE + 1, BLK, LANES), jnp.float32),
            pltpu.SMEM((LATE + 5,), jnp.int32),
            pltpu.SemaphoreType.REGULAR,
            pltpu.SemaphoreType.REGULAR((RING,)),
        ],
        compiler_params=pltpu.CompilerParams(
            collective_id=0, has_side_effects=True, vmem_limit_bytes=56 * 1024 * 1024
        ),
        cost_estimate=pl.CostEstimate(flops=3 * 2**30, bytes_accessed=10 * 2**20, transcendentals=0),
    )(block_cols, psi_low, psi_high.reshape(4, BLK, 256), dip_blocks)


def solution(mesh):
    placed = (P("rows", "jpair"), P("rows", "jpair"), P("rows", None, None), P())
    return jax.shard_map(
        shards, mesh=mesh, in_specs=placed, out_specs=P("rows", "jpair"), check_vma=False
    )
```
